32 devices in a mesh: row: 8 (over z, y), col: 4 (over x, core).
Axes of the slice: x: 2, y: 2, z: 4, core: 2. Of those that a mesh axis runs over, the one named last changes fastest.
Arguments:
- velocity: float32 [3, 128, 256, 1024], P(None, 'col', 'row'), may hold values from -6 to 6
- derivative_x: float32 [1024, 1024], replicated, may hold values from -4 to 4, as said below
- derivative_y: float32 [256, 256], replicated, may hold values from -4 to 4, as said below
- derivative_z: float32 [128, 128], replicated, may hold values from -4 to 4, as said below
- smoothing_x: float32 [1024, 1024], replicated, may hold values from -2 to 2, as said below
- smoothing_y: float32 [256, 256], replicated, may hold values from -2 to 2, as said below
- smoothing_z: float32 [128, 128], replicated, may hold values from -2 to 2, as said below
Outputs:
- filtered_velocity: float32 [3, 128, 256, 1024], P(None, 'col', 'row')
The draws below stay inside these ranges and needn't reach their ends.
Inputs may be any that keep to these rules, and one draw needn't show every extreme that they name: derivative_x is diag(m) times the inverse of the periodic tridiagonal matrix with 1 on the diagonal and 9/20 beside it, times the periodic stencil 63/80 (f[i+1] - f[i-1]) + 9/100 (f[i+2] - f[i-2]) - 7/1200 (f[i+3] - f[i-3]); m holds one positive metric factor per grid line. `derivative_y`: as derivative_x, for the y lines. smoothing_x is the inverse of the periodic tridiagonal matrix with 1 on the diagonal and a[i] beside it in row i, times the periodic filter stencil of row i, whose weights are: at offset 0, 11/16 plus 5/8 times a[i]; at offsets -1 and 1 each, 15/64 plus 17/32 times a[i]; at offsets -2 and 2 each, -3/32 plus 3/16 times a[i]; at offsets -3 and 3 each, 1/64 minus 1/32 times a[i]; each a[i] lies in 0.44 to 0.499. `derivative_z`: as derivative_x, for the z lines. `smoothing_y`: as smoothing_x, for the y lines. `smoothing_z`: as smoothing_x, for the z lines.
All inputs are finite; a program needn't handle non-finite values.
Results may differ from the reference program's by a relative error of at most 0.000082.
Values sent between devices are 32-bit elements; how exact they have to be, the bound alone decides.
No kernel may reach another device: no remote copies, remote signals or barrier semaphores. Data moves between devices by JAX's collectives and lax.ppermute only.
A program may use at most 192 MiB of HBM per device.

```python
import math
import jax
import jax.numpy as jnp
from jax import lax

NX = 1024
NY = 256
NZ = 128


def shifted_eye(count, offset):
    return jnp.roll(jnp.eye(count, dtype=jnp.float32), offset, axis=1)


def pade_matrix(key, count):
    metric = jnp.exp(jax.random.uniform(key, (count,), jnp.float32, math.log(0.6), math.log(1.6)))
    left = jnp.eye(count, dtype=jnp.float32) + (shifted_eye(count, 1) + shifted_eye(count, -1)) * (9.0 / 20.0)
    right = 63.0 / 80.0 * (shifted_eye(count, 1) - shifted_eye(count, -1))
    right = right + 9.0 / 100.0 * (shifted_eye(count, 2) - shifted_eye(count, -2))
    right = right - 7.0 / 1200.0 * (shifted_eye(count, 3) - shifted_eye(count, -3))
    return metric[:, None] * jnp.linalg.solve(left, right)


def filter_matrix(key, count):
    alpha = jax.random.uniform(key, (count,), jnp.float32, 0.44, 0.495)
    coef_zero = (11.0 + 10.0 * alpha) / 16.0
    coef_one = (15.0 + 34.0 * alpha) / 64.0
    coef_two = (-3.0 + 6.0 * alpha) / 32.0
    coef_three = (1.0 - 2.0 * alpha) / 64.0
    left = jnp.eye(count, dtype=jnp.float32) + alpha[:, None] * (shifted_eye(count, 1) + shifted_eye(count, -1))
    right = coef_zero[:, None] * jnp.eye(count, dtype=jnp.float32)
    right = right + coef_one[:, None] * (shifted_eye(count, 1) + shifted_eye(count, -1))
    right = right + coef_two[:, None] * (shifted_eye(count, 2) + shifted_eye(count, -2))
    right = right + coef_three[:, None] * (shifted_eye(count, 3) + shifted_eye(count, -3))
    return jnp.linalg.solve(left, right)


def draw_derivative_x(key, part):
    return pade_matrix(jax.random.fold_in(key, 11), NX)


def draw_derivative_y(key, part):
    return pade_matrix(jax.random.fold_in(key, 12), NY)


def draw_derivative_z(key, part):
    return pade_matrix(jax.random.fold_in(key, 13), NZ)


def draw_smoothing_x(key, part):
    return filter_matrix(jax.random.fold_in(key, 21), NX)


def draw_smoothing_y(key, part):
    return filter_matrix(jax.random.fold_in(key, 22), NY)


def draw_smoothing_z(key, part):
    return filter_matrix(jax.random.fold_in(key, 23), NZ)


def block_levels(own_key, shape, split, least, top_value):
    def one(axis_at, shards_of):
        draws = jax.random.uniform(jax.random.fold_in(jax.random.fold_in(own_key, 6), axis_at), (shards_of,), jnp.float32, least / len(split), top_value / len(split))
        return jnp.repeat(jnp.exp(draws), shape[axis_at] // shards_of).reshape((-1,) + (1,) * (len(shape) - axis_at - 1))

    loudness = one(*split[0])
    for cut in split[1:]:
        loudness = loudness * one(*cut)
    return loudness


def noise(key, dims, width, reach, shards=(), kind=jnp.bfloat16):
    entries = width * jax.random.normal(key, dims, jnp.float32)
    if shards:
        entries = entries * block_levels(key, dims, shards, -0.22, 0.18)
    return jnp.clip(entries, -reach, reach).astype(kind)


def setup_inputs(seed: int = 0) -> dict:
    arg_keys = jax.random.split(jax.random.key(seed), 8)
    velocity = noise(arg_keys[0], (3, NZ, NY, NX), 1.0, 6.0, ((1, 4), (2, 8)), jnp.float32)
    derivative_x = draw_derivative_x(jax.random.fold_in(arg_keys[7], 71), 0)
    derivative_y = draw_derivative_y(jax.random.fold_in(arg_keys[7], 71), 0)
    derivative_z = draw_derivative_z(jax.random.fold_in(arg_keys[7], 71), 0)
    smoothing_x = draw_smoothing_x(jax.random.fold_in(arg_keys[7], 71), 0)
    smoothing_y = draw_smoothing_y(jax.random.fold_in(arg_keys[7], 71), 0)
    smoothing_z = draw_smoothing_z(jax.random.fold_in(arg_keys[7], 71), 0)
    return {"velocity": velocity, "derivative_x": derivative_x, "derivative_y": derivative_y, "derivative_z": derivative_z, "smoothing_x": smoothing_x, "smoothing_y": smoothing_y, "smoothing_z": smoothing_z}


def apply_x(matrix, field):
    return jnp.einsum('xk,czyk->czyx', matrix, field, precision=lax.Precision.HIGHEST)

def apply_y(matrix, field):
    return jnp.einsum('yk,czkx->czyx', matrix, field, precision=lax.Precision.HIGHEST)

def apply_z(matrix, field):
    return jnp.einsum('zk,ckyx->czyx', matrix, field, precision=lax.Precision.HIGHEST)

def reference(velocity, derivative_x, derivative_y, derivative_z, smoothing_x, smoothing_y, smoothing_z):
    tendency = -(apply_x(derivative_x, velocity * velocity[0:1]) + apply_y(derivative_y, velocity * velocity[1:2]) + apply_z(derivative_z, velocity * velocity[2:3]))
    advanced = velocity + 0.1 * tendency
    smooth = apply_y(smoothing_y, advanced)
    smooth = apply_z(smoothing_z, smooth)
    return apply_x(smoothing_x, smooth)
```

```python
import functools

import jax
import jax.numpy as jnp
import numpy as np
from jax import lax
from jax.experimental import pallas as pl
from jax.experimental.pallas import tpu as pltpu
from jax.sharding import PartitionSpec as P

STEP = 0.1
PADE = 9.0 / 20.0
PADE_STENCIL = (63.0 / 80.0, 9.0 / 100.0, -7.0 / 1200.0)
SPAN = 128
LANES = 256
DEPTH = 256
ROWS = 128
TILE = 256
MIB = 1024 * 1024


def numpy_lanes(blocks):
    index = np.arange(SPAN)[None, :]

    def flip(value, level):
        return value[:, index[0] ^ (1 << level)]

    def pick(level, own_right, own_left):
        return np.where((index >> level) & 1 == 1, own_right, own_left)

    return flip, pick


def kernel_lanes(blocks):
    index = lax.broadcasted_iota(jnp.int32, (1, SPAN), 1)

    def pick(level, own_right, own_left):
        return jnp.where((index >> level) & 1 == 1, own_right, own_left)

    def flip(value, level):
        step = 1 << level
        return pick(level, pltpu.roll(value, step, 1), pltpu.roll(value, SPAN - step, 1))

    return flip, pick


def chain_tables(flip, pick, alpha, beta, gamma, delta, blocks):
    levels = blocks.bit_length() - 1
    zero = alpha * 0.0
    unit = zero + 1.0
    width = 2 * levels

    def combine(terms):
        terms = list(terms)
        return [sum(c * v[j] for c, v in terms) for j in range(width)]

    def spot(at):
        return [unit if j == at else zero for j in range(width)]

    def choose(level, own_right, own_left):
        return [pick(level, r, l) for r, l in zip(own_right, own_left)]

    coefs = [alpha, beta, gamma, delta]
    h_own, k_own = [zero] * width, [zero] * width
    merges, saved = [], []
    for level in range(levels):
        sibling = [flip(value, level) for value in coefs]
        h_sib, k_sib = spot(2 * level), spot(2 * level + 1)
        saved.append((coefs, sibling, h_own, k_own, h_sib, k_sib))
        if level == levels - 1:
            break
        a1, b1, g1, d1 = choose(level, sibling, coefs)
        a2, b2, g2, d2 = choose(level, coefs, sibling)
        scale = 1.0 / (1.0 - d1 * a2)
        h_h2, h_k1 = b1 * scale, b1 * scale * a2
        k_k1, k_h2 = g2 * scale, g2 * scale * d1
        own_left = [unit, h_k1, h_h2, zero, zero, k_k1, k_h2, unit]
        own_right = [h_h2, zero, unit, h_k1, k_h2, unit, zero, k_k1]
        merge = choose(level, own_right, own_left)
        merges.append(merge)
        planes = (h_own, k_own, h_sib, k_sib)
        h_own, k_own = combine(zip(merge[:4], planes)), combine(zip(merge[4:], planes))
        coefs = [a1 + b1 * scale * a2 * g1, b1 * scale * b2, g2 * scale * g1, d2 + g2 * scale * d1 * b2]
    (ao, bo, go, do), (ab, bb, gb, db), h_o, k_o, h_b, k_b = saved[-1]
    m00 = 1.0 - (gb * go + db * ao)
    m01 = -(gb * do + db * bo)
    m10 = -(ab * go + bb * ao)
    m11 = 1.0 - (ab * do + bb * bo)
    inverse = 1.0 / (m00 * m11 - m01 * m10)
    right0 = combine([(unit, k_b), (gb, k_o), (db, h_o)])
    right1 = combine([(unit, h_b), (ab, k_o), (bb, h_o)])
    g_in = combine([(inverse * m11, right0), (-inverse * m01, right1)])
    h_in = combine([(inverse * m00, right1), (-inverse * m10, right0)])
    for level in range(levels - 2, -1, -1):
        (ao, bo, go, do), (ab, bb, gb, db), h_o, k_o, h_b, k_b = saved[level]
        left = 1.0 / (1.0 - do * ab)
        right = 1.0 / (1.0 - db * ao)
        h_left = combine([(left, h_b), (left * ab, k_o), (left * ab * go, g_in), (left * bb, h_in)])
        g_right = combine([(right, k_b), (right * gb, g_in), (right * db, h_o), (right * db * bo, h_in)])
        h_in, g_in = choose(level, h_in, h_left), choose(level, g_right, g_in)
    if blocks == 4:
        merge = [flip(value, 1) for value in merges[0]]

        def raw(end):
            over = [end[2] * merge[j] + end[3] * merge[4 + j] for j in range(4)]
            return end[:2] + over[2:] + over[:2]

        return raw(g_in) + raw(h_in)
    return sum(merges, []) + g_in + h_in


def table_counts(blocks):
    levels = blocks.bit_length() - 1
    return (0, 6) if blocks == 4 else (8 * (levels - 1), 2 * levels)


def end_rows(a_past, stencil_past, sign):
    a1, a2, a3 = a_past
    (p1, p2, p3), (_, q2, q3), (_, _, s3) = stencil_past
    zero = p1 * 0.0
    r1 = [sign * p1, sign * p2, sign * p3]
    r2 = [sign * q2, sign * q3, zero]
    w2 = [sign * s3 / a3, zero, zero]
    w1 = [(x - y) / a2 for x, y in zip(r2, w2)]
    w0 = [(x - y) / a1 - z for x, y, z in zip(r1, w1, w2)]
    return w0, w1, w2


def functionals(xp, index, a, a_left, a_right, stencils, symmetric, first_row, last_row):
    n = a.shape[0]
    low = 1.0 if symmetric else -1.0
    past = lambda rows: tuple(stencils(r)[1:] for r in rows)
    right = end_rows(a_right, past(a_right), low)
    left = end_rows(a_left, past(a_left), 1.0)
    at = lambda i, value: xp.where(index == i, value, 0.0)
    centre, *bands = stencils(a)

    def end(row):
        total = centre * row
        for k, band in enumerate(bands, 1):
            part = band * row
            edge = xp.zeros_like(part[:k])
            total = total + xp.concatenate([edge, part[:-k]], axis=0)
            total = total + low * xp.concatenate([part[k:], edge], axis=0)
        for i in range(3):
            moved = row[n - 1 : n] * (right[0][i] + a[n - 1 : n] * right[1][i]) + row[n - 2 : n - 1] * a[n - 2 : n - 1] * right[0][i]
            total = total - at(n - 1 - i, moved)
            moved = row[0:1] * (left[0][i] + a[0:1] * left[1][i]) + row[1:2] * a[1:2] * left[0][i]
            total = total - at(i, moved)
        return total

    tail = lambda w: sum(at(n - 1 - i, c) for i, c in enumerate(w))
    head = lambda w: sum(at(i, c) for i, c in enumerate(w))
    return [tail(right[1]), tail(right[2]), head(left[1]), head(left[2]), end(first_row), end(last_row)]


def pade_line(count, blocks):
    n = count // blocks
    full = np.eye(count) + PADE * (np.eye(count, k=1) + np.eye(count, k=-1))
    full[0, -1] = full[-1, 0] = PADE
    band = np.zeros((count, count))
    for k, c in enumerate(PADE_STENCIL, 1):
        band += c * (np.roll(np.eye(count), k, axis=1) - np.roll(np.eye(count), -k, axis=1))
    beside = np.linalg.solve(full, band)[0, 1]
    inside = np.linalg.inv(np.eye(n) + PADE * (np.eye(n, k=1) + np.eye(n, k=-1)))
    stencils = lambda a: [a * 0.0] + [a * 0.0 + c for c in PADE_STENCIL]
    side = [np.full((1, 1), PADE)] * 3
    index = np.arange(n)[:, None]
    taps = functionals(
        np, index, np.full((n, 1), PADE), side, side, stencils, False, inside[0][:, None], inside[-1][:, None]
    )
    spread = np.stack([-PADE * inside[:, 0], -PADE * inside[:, -1]], axis=1)
    every = lambda value: np.full((1, SPAN), value)
    flip, pick = numpy_lanes(blocks)
    table = chain_tables(
        flip, pick, every(spread[0, 0]), every(spread[0, 1]), every(spread[-1, 0]), every(spread[-1, 1]), blocks
    )
    return beside, np.concatenate(taps, axis=1), spread, np.concatenate(table, axis=0)


def exact_dot(x, y):
    return jnp.dot(x, y, precision=lax.Precision.HIGHEST, preferred_element_type=jnp.float32)


def iota(shape, axis):
    return lax.broadcasted_iota(jnp.int32, shape, axis)


def place_of(lane, n, group, inner):
    return (lane // group, lane % group) if inner else (lane % n, lane // n)


def block_rows(matrix_ref, block, n):
    return matrix_ref[pl.ds(pl.multiple_of(block * n, 8), n), :]


def store_stack(out_ref, rows, taps, block, n, group, inner):
    wide = n * group
    count = rows.shape[1]
    place, line = place_of(iota((1, wide), 1), n, group, inner)
    tiled = exact_dot(rows, (iota((count, wide), 0) == block * n + place).astype(jnp.float32))
    if inner:
        whole = jnp.broadcast_to(tiled[:, None, :], (n, group, wide)).reshape(wide, wide)
    else:
        whole = jnp.concatenate([tiled] * group, axis=0)
    _, row_line = place_of(iota((wide, 1), 0), n, group, inner)
    whole = jnp.where(row_line == line, whole, 0.0)
    mask = iota((group, wide), 0) == line
    both = jnp.concatenate([whole] + [jnp.where(mask, tap, 0.0) for tap in taps], axis=0)
    high = both.astype(jnp.bfloat16)
    half = both.shape[0]
    out_ref[:half] = high
    out_ref[half:] = (both - high.astype(jnp.float32)).astype(jnp.bfloat16)


def ordered(odd, taps):
    r1, r2, l1, l2, h, k = taps
    pick = lambda x, y: jnp.where(odd, x, y)
    return [pick(l1, r1), pick(l2, r2), h, k, pick(r1, l1), pick(r2, l2)]


def store_table(out_ref, odd, spread, factor):
    _, n, lanes = out_ref.shape
    row = iota((n, lanes), 0)
    side = odd.astype(jnp.int32)
    for j in range(2):
        out_ref[j] = jnp.broadcast_to(spread[j] * factor, (n, lanes))
        for k, first in enumerate((side, 1 - side)):
            spot = row == first * j + (1 - first) * (n - 1 - j)
            out_ref[2 + 2 * k + j] = jnp.where(spot, factor, 0.0)


def store_chain(out_ref, rows, block):
    own = jnp.sum(jnp.where(iota(rows.shape, 1) == block, rows, 0.0), axis=1, keepdims=True)
    out_ref[...] = jnp.broadcast_to(own, out_ref.shape)


def derivative_kernel(lines, pos_ref, *refs):
    refs = list(refs)
    take = lambda k: [refs.pop(0) for _ in range(k)]
    matrices, tap_refs, spreads, chain_refs = (take(len(lines)) for _ in range(4))
    stacks, tables, chains = (take(len(lines)) for _ in range(3))
    for axis, (n, group, inner, beside) in enumerate(lines):
        block = pos_ref[axis]
        odd = block % 2 == 1
        rows = block_rows(matrices[axis], block, n)
        count = rows.shape[1]
        next_one = iota((n, count), 1) == (block * n + iota((n, count), 0) + 1) % count
        metric = jnp.sum(jnp.where(next_one, rows, 0.0), axis=1, keepdims=True) * (1.0 / beside)
        taps = [tap_refs[axis][j : j + 1, :] for j in range(6)]
        store_stack(stacks[axis], -STEP * rows, ordered(odd, taps), block, n, group, inner)
        spread = [spreads[axis][:, j : j + 1] for j in range(2)]
        store_table(tables[axis], odd, spread, -STEP * metric)
        store_chain(chains[axis], chain_refs[axis][...], block)


def filter_stencils(a):
    return [
        11.0 / 16.0 + 5.0 / 8.0 * a,
        15.0 / 64.0 + 17.0 / 32.0 * a,
        -3.0 / 32.0 + 3.0 / 16.0 * a,
        1.0 / 64.0 - 1.0 / 32.0 * a,
    ]


def block_ends(a, out_ref):
    n = a.shape[0]
    a = [a[i : i + 1, :] for i in range(n)]
    down, up = [jnp.ones_like(a[0])], [jnp.ones_like(a[0])]
    for i in range(1, n):
        down.append(1.0 / (1.0 - a[i] * a[i - 1] * down[i - 1]))
        j = n - 1 - i
        up.insert(0, 1.0 / (1.0 - a[j] * a[j + 1] * up[0]))
    column = row = up[0]
    out_ref[0, 0:1, :] = column
    out_ref[2, 0:1, :] = row
    for i in range(1, n):
        column = -a[i] * up[i] * column
        row = -a[i - 1] * up[i] * row
        out_ref[0, i : i + 1, :] = column
        out_ref[2, i : i + 1, :] = row
    column = row = down[-1]
    out_ref[1, n - 1 : n, :] = column
    out_ref[3, n - 1 : n, :] = row
    for i in range(n - 2, -1, -1):
        column = -a[i] * down[i] * column
        row = -a[i + 1] * down[i] * row
        out_ref[1, i : i + 1, :] = column
        out_ref[3, i : i + 1, :] = row


def smoothing_kernel(lines, pos_ref, *refs):
    refs = list(refs)
    take = lambda k: [refs.pop(0) for _ in range(k)]
    matrices = take(len(lines))
    stacks, tables, chains = take(len(lines)), take(len(lines)), take(len(lines))
    scratch = take(len(lines))
    for axis, (n, group, inner, blocks) in enumerate(lines):
        block = pos_ref[axis]
        odd = block % 2 == 1
        matrix = matrices[axis][...]
        count = matrix.shape[0]
        row, lane = iota((count, count), 0), iota((count, count), 1)
        middle = jnp.sum(jnp.where(row == lane, matrix, 0.0), axis=0, keepdims=True)
        near = (row == (lane + 1) % count) | (lane == (row + 1) % count)
        beside = jnp.sum(jnp.where(near, matrix, 0.0), axis=0, keepdims=True)
        along = (11.0 / 16.0 - middle) / (beside - 5.0 / 8.0)
        sorted_out = jnp.where(iota((n, count), 1) % n == iota((n, count), 0), along, 0.0)
        a = exact_dot(sorted_out, (iota((count, SPAN), 0) // n == iota((count, SPAN), 1)).astype(jnp.float32))
        ends_ref = scratch[axis]
        block_ends(a, ends_ref)
        column0, column1, row0, row1 = (ends_ref[j] for j in range(4))
        first, last = a[0:1], a[n - 1 : n]
        spread = [-first * column0, -last * column1]
        flip, pick = kernel_lanes(blocks)
        chain = chain_tables(
            flip, pick, spread[0][0:1], spread[1][0:1], spread[0][n - 1 : n], spread[1][n - 1 : n], blocks
        )
        store_chain(chains[axis], jnp.concatenate(chain, axis=0), block)
        index = iota((1, SPAN), 1)
        after = lambda v: jnp.where(index == blocks - 1, pltpu.roll(v, blocks - 1, 1), pltpu.roll(v, SPAN - 1, 1))
        before = lambda v: jnp.where(index == 0, pltpu.roll(v, SPAN - blocks + 1, 1), pltpu.roll(v, 1, 1))
        a_right = [after(a[i : i + 1]) for i in range(3)]
        a_left = [before(a[n - 1 - i : n - i]) for i in range(3)]
        used = index < blocks
        a_right = [jnp.where(used, v, 0.44) for v in a_right]
        a_left = [jnp.where(used, v, 0.44) for v in a_left]
        taps = functionals(jnp, iota((n, SPAN), 0), a, a_left, a_right, filter_stencils, True, row0, row1)
        own = lambda v: jnp.sum(jnp.where(iota((n, SPAN), 1) == block, v, 0.0), axis=1, keepdims=True)
        wide = n * group
        place, _ = place_of(iota((1, wide), 1), n, group, inner)
        at_place = iota((n, wide), 0) == place
        tap_rows = [jnp.sum(jnp.where(at_place, own(t), 0.0), axis=0, keepdims=True) for t in taps]
        rows = block_rows(matrices[axis], block, n)
        store_stack(stacks[axis], rows, ordered(odd, tap_rows), block, n, group, inner)
        store_table(tables[axis], odd, [own(s) for s in spread], jnp.ones((n, 1), jnp.float32))


def stack_shape(n, group):
    return jax.ShapeDtypeStruct((2 * group * (n + 6), group * n), jnp.bfloat16)


def derivative_call(pos, matrices, lines):
    ready = [pade_line(m.shape[0], blocks) for m, (_, _, _, blocks) in zip(matrices, lines)]
    expanded = []
    for (n, group, inner, _), (_, taps, _, _) in zip(lines, ready):
        place, _ = place_of(np.arange(n * group), n, group, inner)
        expanded.append(jnp.asarray(taps[place].T.astype(np.float32)))
    spreads = [jnp.asarray(spread.astype(np.float32)) for _, _, spread, _ in ready]
    chains = [jnp.asarray(table.astype(np.float32)) for _, _, _, table in ready]
    setup = [(n, group, inner, beside) for (n, group, inner, _), (beside, _, _, _) in zip(lines, ready)]
    out = pl.pallas_call(
        functools.partial(derivative_kernel, setup),
        in_specs=[SMEM] + [VMEM] * (4 * len(lines)),
        out_shape=[stack_shape(n, group) for n, group, _, _ in lines]
        + [shape_of(6, n, SPAN) for n, _, _, _ in lines]
        + [shape_of(*chain.shape) for chain in chains],
        compiler_params=params(32),
        name="derivative_lines",
    )(pos, *matrices, *expanded, *spreads, *chains)
    k = len(lines)
    return out[:k], out[k : 2 * k], out[2 * k :]


def smoothing_call(pos, matrices, lines):
    rows = [merged + 2 * planes for merged, planes in (table_counts(blocks) for _, _, _, blocks in lines)]
    out = pl.pallas_call(
        functools.partial(smoothing_kernel, lines),
        in_specs=[SMEM] + [VMEM] * len(lines),
        out_shape=[stack_shape(n, group) for n, group, _, _ in lines]
        + [shape_of(6, n, SPAN) for n, _, _, _ in lines]
        + [shape_of(r, SPAN) for r in rows],
        scratch_shapes=[pltpu.VMEM((4, n, SPAN), jnp.float32) for n, _, _, _ in lines],
        compiler_params=params(32),
        name="smoothing_lines",
    )(pos, *matrices)
    k = len(lines)
    return out[:k], out[k : 2 * k], out[2 * k :]


def split(values):
    high = values.astype(jnp.bfloat16)
    return high, (values - high.astype(jnp.float32)).astype(jnp.bfloat16)


def times(stack, values):
    half = stack.shape[0] // 2
    high, low = split(values)
    dot = functools.partial(jnp.dot, preferred_element_type=jnp.float32)
    first = dot(stack, high)
    return first[:half] + first[half:] + dot(stack[:half], low)


def put_taps(taps, group, at, writers):
    for j, targets in enumerate(writers):
        for ref, plane in targets:
            ref[plane, at : at + group, :] = taps[j * group : (j + 1) * group]


def writers_of(outs, blocks):
    if blocks == 4:
        near, away, ends = outs
        return [
            [(near, 0)],
            [(near, 1)],
            [(near, 2), (away, 2), (ends, 0)],
            [(near, 3), (away, 3), (ends, 1)],
            [(away, 0)],
            [(away, 1)],
        ]
    near, away = outs
    return [[(near, j)] for j in range(4)] + [[(away, j)] for j in range(2)]


def out_planes(blocks):
    return [4, 4, 2] if blocks == 4 else [4, 2]


def along_y(stack, read, count_z, count_y, write, writers):
    group = min(count_z, DEPTH // count_y)
    for at in range(0, count_z, group):
        values = read(slice(at, at + group), slice(0, count_y))
        result = times(stack, values.reshape(group * count_y, -1))
        write(slice(at, at + group), slice(0, count_y), result[: group * count_y].reshape(values.shape))
        put_taps(result[group * count_y :], group, at, writers)


def along_z(stack, read, count_z, count_y, write, writers):
    group = min(count_y, DEPTH // count_z)
    for at in range(0, count_y, group):
        values = read(slice(0, count_z), slice(at, at + group))
        result = times(stack, values.reshape(count_z * group, -1))
        write(slice(0, count_z), slice(at, at + group), result[: count_z * group].reshape(values.shape))
        put_taps(result[count_z * group :], group, at, writers)


def flux_kernel(blocks_y, blocks_z, v_ref, ly_ref, lz_ref, t_ref, *outs):
    count_c, count_z, count_y, _ = v_ref.shape
    outs = list(outs)
    for c in range(count_c):
        outs_y = [outs.pop(0) for _ in out_planes(blocks_y)]
        outs_z = [outs.pop(0) for _ in out_planes(blocks_z)]

        def write_y(zs, ys, value, c=c):
            t_ref[c, zs, ys] = v_ref[c, zs, ys] + value

        def write_z(zs, ys, value, c=c):
            t_ref[c, zs, ys] += value

        flux = lambda k: lambda zs, ys: v_ref[c, zs, ys] * v_ref[k, zs, ys]
        along_y(ly_ref[...], flux(1), count_z, count_y, write_y, writers_of(outs_y, blocks_y))
        along_z(lz_ref[...], flux(2), count_z, count_y, write_z, writers_of(outs_z, blocks_z))


def ends_of(chain_ref, blocks, planes):
    merged, count = table_counts(blocks)
    weight = lambda i, j: chain_ref[merged + i * count + j : merged + i * count + j + 1, :]
    return [sum(weight(i, j) * plane for j, plane in enumerate(planes)) for i in range(2)]


def spans(width):
    return [slice(x, x + SPAN) for x in range(0, width, SPAN)]


def far_planes(parts, blocks, xs):
    if blocks == 4:
        near, away, opposite = parts
        return [near[2, :, xs], near[3, :, xs], away[2, :, xs], away[3, :, xs], opposite[0, :, xs], opposite[1, :, xs]]
    near, _, *rest = parts
    return [near[2, :, xs], near[3, :, xs]] + [ref[j, :, xs] for ref in rest for j in range(2)]


def mend_y(read, write, chain_ref, table_ref, parts, blocks, ends_ref, dims):
    count_z, count_y, width = dims
    near, away = parts[:2]
    for xs in spans(width):
        ends_ref[0], ends_ref[1] = ends_of(chain_ref, blocks, far_planes(parts, blocks, xs))
        for y in range(0, count_y, 8):
            ys = slice(y, y + 8)
            column = [table_ref[j, ys, :] for j in range(6)]
            for z in range(count_z):
                at = slice(z, z + 1)
                value = read(z, ys, xs) + column[0] * ends_ref[0, at, :] + column[1] * ends_ref[1, at, :]
                if y == 0 or y == count_y - 8:
                    value = value + column[2] * near[0, at, xs] + column[3] * near[1, at, xs]
                    value = value + column[4] * away[0, at, xs] + column[5] * away[1, at, xs]
                write(z, ys, xs, value)


def mend_z(read, write, chain_ref, table_ref, parts, blocks, count_z, width):
    near, away = parts[:2]
    for xs in spans(width):
        g, h = ends_of(chain_ref, blocks, far_planes(parts, blocks, xs))
        for z in range(count_z):
            factor = [table_ref[j, z : z + 1, :] for j in range(6)]
            value = read(z, xs) + factor[0] * g + factor[1] * h
            if z in (0, count_z - 1):
                value = value + factor[2] * near[0, :, xs] + factor[4] * away[0, :, xs]
            if z in (1, count_z - 2):
                value = value + factor[3] * near[1, :, xs] + factor[5] * away[1, :, xs]
            write(z, xs, value)


def advance_kernel(blocks_y, blocks_z, *refs):
    refs = list(refs)
    take = lambda n: [refs.pop(0) for _ in range(n)]
    t_ref, lz_ref, cy_ref, cz_ref, sy_ref, sz_ref = take(6)
    y_parts, z_parts = take(part_count(blocks_y)), take(part_count(blocks_z))
    (out_ref,) = take(1)
    outs = take(len(out_planes(blocks_z)))
    whole, ends = take(2)
    _, count_z, count_y, width = t_ref.shape

    def store_y(z, ys, xs, value):
        whole[z, ys, xs] = value

    def store_z(z, xs, value):
        whole[z, :, xs] = value

    def write(zs, ys, value):
        out_ref[zs, ys] = value

    dims = (count_z, count_y, width)
    mend_y(lambda z, ys, xs: t_ref[0, z, ys, xs], store_y, cy_ref, sy_ref, y_parts, blocks_y, ends, dims)
    mend_z(lambda z, xs: whole[z, :, xs], store_z, cz_ref, sz_ref, z_parts, blocks_z, count_z, width)
    along_z(lz_ref[...], lambda zs, ys: whole[zs, ys], count_z, count_y, write, writers_of(outs, blocks_z))


def filter_kernel(blocks_y, blocks_z, *refs):
    refs = list(refs)
    take = lambda n: [refs.pop(0) for _ in range(n)]
    t_ref, ly_ref, cz_ref, sz_ref = take(4)
    z_parts = take(part_count(blocks_z))
    (out_ref,) = take(1)
    outs = take(len(out_planes(blocks_y)))
    (whole,) = take(1)
    count_z, count_y, width = t_ref.shape

    def store_z(z, xs, value):
        whole[z, :, xs] = value

    def write(zs, ys, value):
        out_ref[zs, ys] = value

    mend_z(lambda z, xs: t_ref[z, :, xs], store_z, cz_ref, sz_ref, z_parts, blocks_z, count_z, width)
    along_y(ly_ref[...], lambda zs, ys: whole[zs, ys], count_z, count_y, write, writers_of(outs, blocks_y))


def split_once(matrix_ref, high_ref, low_ref, factor):
    @pl.when(pl.program_id(0) == 0)
    def _():
        count = matrix_ref.shape[0]
        step = min(count, 128)
        for at in range(0, count, step):
            high_ref[at : at + step], low_ref[at : at + step] = split(matrix_ref[at : at + step] * factor)


def cut(array, start, count):
    whole = array.shape[1]
    start = start % whole
    if start + count <= whole:
        return array[:, start : start + count]
    return jnp.concatenate([array[:, start:], array[:, : start + count - whole]], axis=1)


def rows_times(values, high_ref, low_ref, write):
    high, low = split(values)
    dot = lambda x, w: lax.dot_general(x, w, (((1,), (1,)), ((), ())), preferred_element_type=jnp.float32)
    width = values.shape[1]
    for at in range(0, width, TILE):
        near = min(width, 2 * TILE)
        start = at - TILE // 2
        w_high, w_low = high_ref[at : at + TILE, :], low_ref[at : at + TILE, :]
        x_near, w_near = cut(high, start, near), cut(w_high, start, near)
        total = dot(x_near, w_near) + (dot(cut(low, start, near), w_near) + dot(x_near, cut(w_low, start, near)))
        if near < width:
            total = total + dot(cut(high, start + near, width - near), cut(w_high, start + near, width - near))
        write(slice(at, at + TILE), total)


def flux_x_kernel(v_ref, t_ref, matrix_ref, out_ref, high_ref, low_ref):
    split_once(matrix_ref, high_ref, low_ref, -STEP)
    values = v_ref[...] * v_ref[0:1]

    def write(xs, value):
        out_ref[:, :, :, xs] = t_ref[:, :, :, xs] + value.reshape(values.shape[:3] + (-1,))

    rows_times(values.reshape(-1, values.shape[-1]), high_ref, low_ref, write)


def last_kernel(blocks_y, aliased, *refs):
    refs = list(refs)
    take = lambda n: [refs.pop(0) for _ in range(n)]
    t_ref, matrix_ref, cy_ref, sy_ref = take(4)
    y_parts = take(part_count(blocks_y))
    take(aliased)
    (out_ref,) = take(1)
    whole, ends, high_ref, low_ref = take(4)
    count_z, count_y, width = t_ref.shape
    split_once(matrix_ref, high_ref, low_ref, 1.0)

    def store_y(z, ys, xs, value):
        whole[z, ys, xs] = value

    dims = (count_z, count_y, width)
    mend_y(lambda z, ys, xs: t_ref[z, ys, xs], store_y, cy_ref, sy_ref, y_parts, blocks_y, ends, dims)

    def write(xs, value):
        out_ref[0, :, :, xs] = value.reshape((count_z, count_y, -1))

    rows_times(whole[...].reshape(-1, width), high_ref, low_ref, write)


def merge_kernel(first_row, offset, chain_ref, own_ref, other_ref, out_ref):
    for xs in spans(out_ref.shape[2]):
        planes = [ref[offset + j, :, xs] for ref in (own_ref, other_ref) for j in range(2)]
        for i in range(2):
            row = first_row + 4 * i
            out_ref[i, :, xs] = sum(chain_ref[row + j : row + j + 1, :] * plane for j, plane in enumerate(planes))


def params(mib):
    return pltpu.CompilerParams(vmem_limit_bytes=mib * MIB)


def shape_of(*dims):
    return jax.ShapeDtypeStruct(dims, jnp.float32)


SMEM = pl.BlockSpec(memory_space=pltpu.SMEM)
VMEM = pl.BlockSpec(memory_space=pltpu.VMEM)


def part_count(blocks):
    return 3 if blocks == 4 else blocks.bit_length()


def whole_spec(array):
    return pl.BlockSpec(array.shape, lambda *_: (0,) * array.ndim)


def lane_spec(dims):
    return pl.BlockSpec(tuple(dims) + (LANES,), lambda i: (0,) * len(dims) + (i,))


def cost(flops, size):
    return pl.CostEstimate(flops=int(flops), bytes_accessed=int(size), transcendentals=0)


def flux_call(velocity, ly, lz, blocks_y, blocks_z):
    nc, nz, ny, width = velocity.shape
    size = nc * nz * ny * width
    planes = [(k, nz) for k in out_planes(blocks_y)] + [(k, ny) for k in out_planes(blocks_z)]
    planes = planes * nc
    out = pl.pallas_call(
        functools.partial(flux_kernel, blocks_y, blocks_z),
        grid=(width // LANES,),
        in_specs=[lane_spec((nc, nz, ny)), whole_spec(ly), whole_spec(lz)],
        out_specs=[lane_spec((nc, nz, ny))] + [lane_spec(dims) for dims in planes],
        out_shape=[shape_of(nc, nz, ny, width)] + [shape_of(*dims, width) for dims in planes],
        compiler_params=params(60),
        cost_estimate=cost(size * 2 * 256 * 8, size * 9),
        name="flux_yz",
    )(velocity, ly, lz)
    each = len(planes) // nc
    first = len(out_planes(blocks_y))
    parts = [out[1 + c * each : 1 + (c + 1) * each] for c in range(nc)]
    return out[0], [(p[:first], p[first:]) for p in parts]


def flux_x_call(velocity, t, matrix, part, parts):
    nc, nz, ny, width = velocity.shape
    group = max(1, min(nz // parts, ROWS // ny))
    steps = nz // parts // group
    block = pl.BlockSpec((nc, group, ny, width), lambda i: (0, part * steps + i, 0, 0))
    size = nc * nz * ny * width // parts
    return pl.pallas_call(
        flux_x_kernel,
        grid=(steps,),
        in_specs=[block, block, whole_spec(matrix)],
        out_specs=block,
        out_shape=shape_of(nc, nz, ny, width),
        scratch_shapes=[pltpu.VMEM(matrix.shape, jnp.bfloat16)] * 2,
        input_output_aliases={1: 0},
        compiler_params=params(60),
        cost_estimate=cost(size * 4 * width, size * 13),
        name="flux_x",
    )(velocity, t, matrix)


def advance_call(t, c, lz, cy, cz, sy, sz, y_parts, z_parts, blocks_y, blocks_z):
    _, nz, ny, width = t.shape
    size = nz * ny * width
    planes = list(y_parts) + list(z_parts)
    outs = [(k, ny) for k in out_planes(blocks_z)]
    component = pl.BlockSpec((1, nz, ny, LANES), lambda i: (c, 0, 0, i))
    return pl.pallas_call(
        functools.partial(advance_kernel, blocks_y, blocks_z),
        grid=(width // LANES,),
        in_specs=[component] + [whole_spec(a) for a in (lz, cy, cz, sy, sz)]
        + [lane_spec(p.shape[:2]) for p in planes],
        out_specs=[lane_spec((nz, ny))] + [lane_spec(dims) for dims in outs],
        out_shape=[shape_of(nz, ny, width)] + [shape_of(*dims, width) for dims in outs],
        scratch_shapes=[pltpu.VMEM((nz, ny, LANES), jnp.float32), pltpu.VMEM((2, nz, SPAN), jnp.float32)],
        compiler_params=params(60),
        cost_estimate=cost(size * 2 * 256 * 4, size * 9),
        name="advance_z",
    )(t, lz, cy, cz, sy, sz, *planes)


def filter_call(t, ly, cz, sz, z_parts, blocks_y, blocks_z):
    nz, ny, width = t.shape
    size = nz * ny * width
    outs = [(k, nz) for k in out_planes(blocks_y)]
    return pl.pallas_call(
        functools.partial(filter_kernel, blocks_y, blocks_z),
        grid=(width // LANES,),
        in_specs=[lane_spec((nz, ny))] + [whole_spec(a) for a in (ly, cz, sz)] + [lane_spec(p.shape[:2]) for p in z_parts],
        out_specs=[lane_spec((nz, ny))] + [lane_spec(dims) for dims in outs],
        out_shape=[shape_of(nz, ny, width)] + [shape_of(*dims, width) for dims in outs],
        scratch_shapes=[pltpu.VMEM((nz, ny, LANES), jnp.float32)],
        compiler_params=params(60),
        cost_estimate=cost(size * 2 * 256 * 4, size * 9),
        name="filter_y",
    )(t, ly, cz, sz, *z_parts)


def last_call(whole, t, c, count_c, matrix, cy, sy, y_parts, blocks_y):
    nz, ny, width = t.shape
    group = max(8, min(nz, DEPTH // ny))
    block = pl.BlockSpec((group, ny, width), lambda i: (i, 0, 0))
    plane = lambda k: pl.BlockSpec((k, group, width), lambda i: (0, i, 0))
    size = nz * ny * width
    aliased = [] if whole is None else [whole]
    operands = [t, matrix, cy, sy, *y_parts, *aliased]
    return pl.pallas_call(
        functools.partial(last_kernel, blocks_y, len(aliased)),
        grid=(nz // group,),
        in_specs=[block] + [whole_spec(a) for a in (matrix, cy, sy)]
        + [plane(p.shape[0]) for p in y_parts]
        + [pl.BlockSpec(memory_space=pl.ANY)] * len(aliased),
        out_specs=pl.BlockSpec((1, group, ny, width), lambda i: (c, i, 0, 0)),
        out_shape=shape_of(count_c, nz, ny, width),
        scratch_shapes=[pltpu.VMEM((group, ny, width), jnp.float32), pltpu.VMEM((2, group, SPAN), jnp.float32)]
        + [pltpu.VMEM(matrix.shape, jnp.bfloat16)] * 2,
        input_output_aliases={len(operands) - 1: 0} if aliased else {},
        compiler_params=params(60),
        cost_estimate=cost(size * 6 * width, size * 13),
        name="filter_x",
    )(*operands)


def merge_call(chain, first_row, own, other):
    offset = own.shape[0] - 2
    dims = own.shape[1:]
    size = 2 * dims[0] * dims[1]
    return pl.pallas_call(
        functools.partial(merge_kernel, first_row, offset),
        in_specs=[VMEM] * 3,
        out_shape=shape_of(2, *dims),
        cost_estimate=cost(size * 8, size * 12),
        name="merge",
    )(chain, own, other)


def exchange(axis, outs, chain):
    blocks = lax.axis_size(axis)
    near_pairs = [(i, i ^ 1) for i in range(blocks)]
    away_pairs = [(i, (i - 1 if i % 2 == 0 else i + 1) % blocks) for i in range(blocks)]
    near = lax.ppermute(outs[0], axis, near_pairs)
    parts = [near, lax.ppermute(outs[1], axis, away_pairs)]
    if blocks == 4:
        return parts + [lax.ppermute(outs[2], axis, [(i, i ^ 2) for i in range(blocks)])]
    own, other = outs[0], near
    for level in range(1, blocks.bit_length() - 1):
        own = merge_call(chain, 8 * (level - 1), own, other)
        other = lax.ppermute(own, axis, [(i, i ^ (1 << level)) for i in range(blocks)])
        parts.append(other)
    return parts


def on_device(velocity, derivative_x, derivative_y, derivative_z, smoothing_x, smoothing_y, smoothing_z):
    num_row, num_col = lax.axis_size("row"), lax.axis_size("col")
    pos = jnp.stack([lax.axis_index("row"), lax.axis_index("col")]).astype(jnp.int32)
    count_c, nz, ny, _ = velocity.shape
    lines = ((ny, min(nz, DEPTH // ny), False, num_row), (nz, min(ny, DEPTH // nz), True, num_col))

    (ly, lz), (dy, dz), (cy, cz) = derivative_call(pos, (derivative_y, derivative_z), lines)
    flux, parts = flux_call(velocity, ly, lz, num_row, num_col)
    flux_parts = [
        (exchange("row", y_outs, cy), exchange("col", z_outs, cz)) for y_outs, z_outs in parts
    ]
    (my, mz), (sy, sz), (fy, fz) = smoothing_call(pos, (smoothing_y, smoothing_z), lines)
    for part in range(2):
        flux = flux_x_call(velocity, flux, derivative_x, part, 2)
    out = None
    for c, (y_parts, z_parts) in enumerate(flux_parts):
        t, *z_outs = advance_call(flux, c, mz, cy, cz, dy, dz, y_parts, z_parts, num_row, num_col)
        z_parts = exchange("col", z_outs, fz)
        t, *y_outs = filter_call(t, my, fz, sz, z_parts, num_row, num_col)
        y_parts = exchange("row", y_outs, fy)
        out = last_call(out, t, c, count_c, smoothing_x, fy, sy, y_parts, num_row)
    return out


def solution(mesh):
    in_specs = (P(None, "col", "row", None), P(), P(), P(), P(), P(), P())
    out_specs = P(None, "col", "row", None)
    return jax.shard_map(
        on_device, mesh=mesh, in_specs=in_specs, out_specs=out_specs, check_vma=False
    )
```

```python
import functools

import jax
import jax.numpy as jnp
import numpy as np
from jax import lax
from jax.experimental import pallas as pl
from jax.experimental.pallas import tpu as pltpu
from jax.sharding import PartitionSpec as P

STEP = 0.1
PADE = 9.0 / 20.0
PADE_STENCIL = (63.0 / 80.0, 9.0 / 100.0, -7.0 / 1200.0)
SPAN = 128
LANES = 256
DEPTH = 256
ROWS = 128
TILE = 256
MIB = 1024 * 1024
SMALL_MIB = 24
ADVANCE_MIB = 50
WEIGHT = 1000


def numpy_lanes(blocks):
    index = np.arange(SPAN)[None, :]

    def flip(value, level):
        return value[:, index[0] ^ (1 << level)]

    def pick(level, own_right, own_left):
        return np.where((index >> level) & 1 == 1, own_right, own_left)

    return flip, pick


def kernel_lanes(blocks):
    index = lax.broadcasted_iota(jnp.int32, (1, SPAN), 1)

    def pick(level, own_right, own_left):
        return jnp.where((index >> level) & 1 == 1, own_right, own_left)

    def flip(value, level):
        step = 1 << level
        return pick(level, pltpu.roll(value, step, 1), pltpu.roll(value, SPAN - step, 1))

    return flip, pick


def chain_tables(flip, pick, alpha, beta, gamma, delta, blocks):
    levels = blocks.bit_length() - 1
    zero = alpha * 0.0
    unit = zero + 1.0
    width = 2 * levels

    def combine(terms):
        terms = list(terms)
        return [sum(c * v[j] for c, v in terms) for j in range(width)]

    def spot(at):
        return [unit if j == at else zero for j in range(width)]

    def choose(level, own_right, own_left):
        return [pick(level, r, l) for r, l in zip(own_right, own_left)]

    coefs = [alpha, beta, gamma, delta]
    h_own, k_own = [zero] * width, [zero] * width
    merges, saved = [], []
    for level in range(levels):
        sibling = [flip(value, level) for value in coefs]
        h_sib, k_sib = spot(2 * level), spot(2 * level + 1)
        saved.append((coefs, sibling, h_own, k_own, h_sib, k_sib))
        if level == levels - 1:
            break
        a1, b1, g1, d1 = choose(level, sibling, coefs)
        a2, b2, g2, d2 = choose(level, coefs, sibling)
        scale = 1.0 / (1.0 - d1 * a2)
        h_h2, h_k1 = b1 * scale, b1 * scale * a2
        k_k1, k_h2 = g2 * scale, g2 * scale * d1
        own_left = [unit, h_k1, h_h2, zero, zero, k_k1, k_h2, unit]
        own_right = [h_h2, zero, unit, h_k1, k_h2, unit, zero, k_k1]
        merge = choose(level, own_right, own_left)
        merges.append(merge)
        planes = (h_own, k_own, h_sib, k_sib)
        h_own, k_own = combine(zip(merge[:4], planes)), combine(zip(merge[4:], planes))
        coefs = [a1 + b1 * scale * a2 * g1, b1 * scale * b2, g2 * scale * g1, d2 + g2 * scale * d1 * b2]
    (ao, bo, go, do), (ab, bb, gb, db), h_o, k_o, h_b, k_b = saved[-1]
    m00 = 1.0 - (gb * go + db * ao)
    m01 = -(gb * do + db * bo)
    m10 = -(ab * go + bb * ao)
    m11 = 1.0 - (ab * do + bb * bo)
    inverse = 1.0 / (m00 * m11 - m01 * m10)
    right0 = combine([(unit, k_b), (gb, k_o), (db, h_o)])
    right1 = combine([(unit, h_b), (ab, k_o), (bb, h_o)])
    g_in = combine([(inverse * m11, right0), (-inverse * m01, right1)])
    h_in = combine([(inverse * m00, right1), (-inverse * m10, right0)])
    for level in range(levels - 2, -1, -1):
        (ao, bo, go, do), (ab, bb, gb, db), h_o, k_o, h_b, k_b = saved[level]
        left = 1.0 / (1.0 - do * ab)
        right = 1.0 / (1.0 - db * ao)
        h_left = combine([(left, h_b), (left * ab, k_o), (left * ab * go, g_in), (left * bb, h_in)])
        g_right = combine([(right, k_b), (right * gb, g_in), (right * db, h_o), (right * db * bo, h_in)])
        h_in, g_in = choose(level, h_in, h_left), choose(level, g_right, g_in)
    return sum(merges, []) + g_in + h_in


def table_counts(blocks):
    levels = blocks.bit_length() - 1
    return 8 * (levels - 1), 2 * levels


def end_rows(a_past, stencil_past, sign):
    a1, a2, a3 = a_past
    (p1, p2, p3), (_, q2, q3), (_, _, s3) = stencil_past
    zero = p1 * 0.0
    r1 = [sign * p1, sign * p2, sign * p3]
    r2 = [sign * q2, sign * q3, zero]
    w2 = [sign * s3 / a3, zero, zero]
    w1 = [(x - y) / a2 for x, y in zip(r2, w2)]
    w0 = [(x - y) / a1 - z for x, y, z in zip(r1, w1, w2)]
    return w0, w1, w2


def functionals(xp, index, a, a_left, a_right, stencils, symmetric, first_row, last_row):
    n = a.shape[0]
    low = 1.0 if symmetric else -1.0
    past = lambda rows: tuple(stencils(r)[1:] for r in rows)
    right = end_rows(a_right, past(a_right), low)
    left = end_rows(a_left, past(a_left), 1.0)
    at = lambda i, value: xp.where(index == i, value, 0.0)
    centre, *bands = stencils(a)

    def end(row):
        total = centre * row
        for k, band in enumerate(bands, 1):
            part = band * row
            edge = xp.zeros_like(part[:k])
            total = total + xp.concatenate([edge, part[:-k]], axis=0)
            total = total + low * xp.concatenate([part[k:], edge], axis=0)
        for i in range(3):
            moved = row[n - 1 : n] * (right[0][i] + a[n - 1 : n] * right[1][i]) + row[n - 2 : n - 1] * a[n - 2 : n - 1] * right[0][i]
            total = total - at(n - 1 - i, moved)
            moved = row[0:1] * (left[0][i] + a[0:1] * left[1][i]) + row[1:2] * a[1:2] * left[0][i]
            total = total - at(i, moved)
        return total

    tail = lambda w: sum(at(n - 1 - i, c) for i, c in enumerate(w))
    head = lambda w: sum(at(i, c) for i, c in enumerate(w))
    return [tail(right[1]), tail(right[2]), head(left[1]), head(left[2]), end(first_row), end(last_row)]


def pade_line(count, blocks):
    n = count // blocks
    full = np.eye(count) + PADE * (np.eye(count, k=1) + np.eye(count, k=-1))
    full[0, -1] = full[-1, 0] = PADE
    band = np.zeros((count, count))
    for k, c in enumerate(PADE_STENCIL, 1):
        band += c * (np.roll(np.eye(count), k, axis=1) - np.roll(np.eye(count), -k, axis=1))
    beside = np.linalg.solve(full, band)[0, 1]
    inside = np.linalg.inv(np.eye(n) + PADE * (np.eye(n, k=1) + np.eye(n, k=-1)))
    stencils = lambda a: [a * 0.0] + [a * 0.0 + c for c in PADE_STENCIL]
    side = [np.full((1, 1), PADE)] * 3
    index = np.arange(n)[:, None]
    taps = functionals(
        np, index, np.full((n, 1), PADE), side, side, stencils, False, inside[0][:, None], inside[-1][:, None]
    )
    spread = np.stack([-PADE * inside[:, 0], -PADE * inside[:, -1]], axis=1)
    every = lambda value: np.full((1, SPAN), value)
    flip, pick = numpy_lanes(blocks)
    table = chain_tables(
        flip, pick, every(spread[0, 0]), every(spread[0, 1]), every(spread[-1, 0]), every(spread[-1, 1]), blocks
    )
    return beside, np.concatenate(taps, axis=1), spread, np.concatenate(table, axis=0)


def exact_dot(x, y):
    return jnp.dot(x, y, precision=lax.Precision.HIGHEST, preferred_element_type=jnp.float32)


def iota(shape, axis):
    return lax.broadcasted_iota(jnp.int32, shape, axis)


def place_of(lane, n, group, inner):
    return (lane // group, lane % group) if inner else (lane % n, lane // n)


def block_rows(matrix_ref, block, n):
    return matrix_ref[pl.ds(pl.multiple_of(block * n, 8), n), :]


def store_stack(out_ref, rows, taps, block, n, group, inner):
    wide = n * group
    count = rows.shape[1]
    place, line = place_of(iota((1, wide), 1), n, group, inner)
    tiled = exact_dot(rows, (iota((count, wide), 0) == block * n + place).astype(jnp.float32))
    if inner:
        whole = jnp.broadcast_to(tiled[:, None, :], (n, group, wide)).reshape(wide, wide)
    else:
        whole = jnp.concatenate([tiled] * group, axis=0)
    _, row_line = place_of(iota((wide, 1), 0), n, group, inner)
    whole = jnp.where(row_line == line, whole, 0.0)
    mask = iota((group, wide), 0) == line
    both = jnp.concatenate([whole] + [jnp.where(mask, tap, 0.0) for tap in taps], axis=0)
    high = both.astype(jnp.bfloat16)
    half = both.shape[0]
    out_ref[:half] = high
    out_ref[half:] = (both - high.astype(jnp.float32)).astype(jnp.bfloat16)


def ordered(odd, taps):
    r1, r2, l1, l2, h, k = taps
    pick = lambda x, y: jnp.where(odd, x, y)
    return [pick(l1, r1), pick(l2, r2), h, k, pick(r1, l1), pick(r2, l2)]


def store_table(out_ref, odd, spread, factor):
    _, n, lanes = out_ref.shape
    row = iota((n, lanes), 0)
    side = odd.astype(jnp.int32)
    for j in range(2):
        out_ref[j] = jnp.broadcast_to(spread[j] * factor, (n, lanes))
        for k, first in enumerate((side, 1 - side)):
            spot = row == first * j + (1 - first) * (n - 1 - j)
            out_ref[2 + 2 * k + j] = jnp.where(spot, factor, 0.0)


def store_chain(out_ref, rows, block):
    own = jnp.sum(jnp.where(iota(rows.shape, 1) == block, rows, 0.0), axis=1, keepdims=True)
    out_ref[...] = jnp.broadcast_to(own, out_ref.shape)


def prepare_derivatives(lines, pos_ref, matrices, constants_ref, stacks, tables, chains):
    for axis, (n, group, inner, beside, (tap_at, spread_at, chain_at, chain_rows)) in enumerate(lines):
        block = pos_ref[axis]
        odd = block % 2 == 1
        rows = block_rows(matrices[axis], block, n)
        count = rows.shape[1]
        next_one = iota((n, count), 1) == (block * n + iota((n, count), 0) + 1) % count
        metric = jnp.sum(jnp.where(next_one, rows, 0.0), axis=1, keepdims=True) * (1.0 / beside)
        taps = [constants_ref[tap_at + j : tap_at + j + 1, : n * group] for j in range(6)]
        store_stack(stacks[axis], -STEP * rows, ordered(odd, taps), block, n, group, inner)
        spread = [constants_ref[spread_at : spread_at + n, j : j + 1] for j in range(2)]
        store_table(tables[axis], odd, spread, -STEP * metric)
        store_chain(chains[axis], constants_ref[chain_at : chain_at + chain_rows, :SPAN], block)


def filter_stencils(a):
    return [
        11.0 / 16.0 + 5.0 / 8.0 * a,
        15.0 / 64.0 + 17.0 / 32.0 * a,
        -3.0 / 32.0 + 3.0 / 16.0 * a,
        1.0 / 64.0 - 1.0 / 32.0 * a,
    ]


def block_ends(a, out_ref):
    n = a.shape[0]
    a = [a[i : i + 1, :] for i in range(n)]
    down, up = [jnp.ones_like(a[0])], [jnp.ones_like(a[0])]
    for i in range(1, n):
        down.append(1.0 / (1.0 - a[i] * a[i - 1] * down[i - 1]))
        j = n - 1 - i
        up.insert(0, 1.0 / (1.0 - a[j] * a[j + 1] * up[0]))
    column = row = up[0]
    out_ref[0, 0:1, :] = column
    out_ref[2, 0:1, :] = row
    for i in range(1, n):
        column = -a[i] * up[i] * column
        row = -a[i - 1] * up[i] * row
        out_ref[0, i : i + 1, :] = column
        out_ref[2, i : i + 1, :] = row
    column = row = down[-1]
    out_ref[1, n - 1 : n, :] = column
    out_ref[3, n - 1 : n, :] = row
    for i in range(n - 2, -1, -1):
        column = -a[i] * down[i] * column
        row = -a[i + 1] * down[i] * row
        out_ref[1, i : i + 1, :] = column
        out_ref[3, i : i + 1, :] = row


def smoothing_kernel(lines, pos_ref, *refs):
    refs = list(refs)
    take = lambda k: [refs.pop(0) for _ in range(k)]
    matrices = take(len(lines))
    stacks, tables, chains = take(len(lines)), take(len(lines)), take(len(lines))
    scratch = take(len(lines))
    for axis, (n, group, inner, blocks) in enumerate(lines):
        block = pos_ref[axis]
        odd = block % 2 == 1
        matrix = matrices[axis][...]
        count = matrix.shape[0]
        row, lane = iota((count, count), 0), iota((count, count), 1)
        middle = jnp.sum(jnp.where(row == lane, matrix, 0.0), axis=0, keepdims=True)
        near = (row == (lane + 1) % count) | (lane == (row + 1) % count)
        beside = jnp.sum(jnp.where(near, matrix, 0.0), axis=0, keepdims=True)
        along = (11.0 / 16.0 - middle) / (beside - 5.0 / 8.0)
        sorted_out = jnp.where(iota((n, count), 1) % n == iota((n, count), 0), along, 0.0)
        a = exact_dot(sorted_out, (iota((count, SPAN), 0) // n == iota((count, SPAN), 1)).astype(jnp.float32))
        ends_ref = scratch[axis]
        block_ends(a, ends_ref)
        column0, column1, row0, row1 = (ends_ref[j] for j in range(4))
        first, last = a[0:1], a[n - 1 : n]
        spread = [-first * column0, -last * column1]
        flip, pick = kernel_lanes(blocks)
        chain = chain_tables(
            flip, pick, spread[0][0:1], spread[1][0:1], spread[0][n - 1 : n], spread[1][n - 1 : n], blocks
        )
        store_chain(chains[axis], jnp.concatenate(chain, axis=0), block)
        index = iota((1, SPAN), 1)
        after = lambda v: jnp.where(index == blocks - 1, pltpu.roll(v, blocks - 1, 1), pltpu.roll(v, SPAN - 1, 1))
        before = lambda v: jnp.where(index == 0, pltpu.roll(v, SPAN - blocks + 1, 1), pltpu.roll(v, 1, 1))
        a_right = [after(a[i : i + 1]) for i in range(3)]
        a_left = [before(a[n - 1 - i : n - i]) for i in range(3)]
        used = index < blocks
        a_right = [jnp.where(used, v, 0.44) for v in a_right]
        a_left = [jnp.where(used, v, 0.44) for v in a_left]
        taps = functionals(jnp, iota((n, SPAN), 0), a, a_left, a_right, filter_stencils, True, row0, row1)
        own = lambda v: jnp.sum(jnp.where(iota((n, SPAN), 1) == block, v, 0.0), axis=1, keepdims=True)
        wide = n * group
        place, _ = place_of(iota((1, wide), 1), n, group, inner)
        at_place = iota((n, wide), 0) == place
        tap_rows = [jnp.sum(jnp.where(at_place, own(t), 0.0), axis=0, keepdims=True) for t in taps]
        rows = block_rows(matrices[axis], block, n)
        store_stack(stacks[axis], rows, ordered(odd, tap_rows), block, n, group, inner)
        store_table(tables[axis], odd, [own(s) for s in spread], jnp.ones((n, 1), jnp.float32))


def stack_shape(n, group):
    return jax.ShapeDtypeStruct((2 * group * (n + 6), group * n), jnp.bfloat16)


def derivative_constants(matrices, lines):
    rows, setup, at = [], [], 0

    def add(value):
        nonlocal at
        start = at
        high = -(-value.shape[0] // 8) * 8
        rows.append(np.pad(value, ((0, high - value.shape[0]), (0, DEPTH - value.shape[1]))))
        at += high
        return start

    for matrix, (n, group, inner, blocks) in zip(matrices, lines):
        beside, taps, spread, table = pade_line(matrix.shape[0], blocks)
        place, _ = place_of(np.arange(n * group), n, group, inner)
        where = (add(taps[place].T), add(spread), add(table), table.shape[0])
        setup.append((n, group, inner, beside, where))
    return jnp.asarray(np.concatenate(rows, axis=0).astype(np.float32)), setup


def smoothing_call(order, pos, matrices, lines):
    rows = [merged + 2 * planes for merged, planes in (table_counts(blocks) for _, _, _, blocks in lines)]
    out, _ = order.call(
        functools.partial(smoothing_kernel, lines),
        [pos, *matrices],
        [SMEM] + [VMEM] * len(lines),
        [VMEM] * (3 * len(lines)),
        [stack_shape(n, group) for n, group, _, _ in lines]
        + [shape_of(6, n, SPAN) for n, _, _, _ in lines]
        + [shape_of(r, SPAN) for r in rows],
        scratch_shapes=[pltpu.VMEM((4, n, SPAN), jnp.float32) for n, _, _, _ in lines],
        compiler_params=params(SMALL_MIB),
        cost_estimate=cost(10**7, 10**7),
        name="smoothing_lines",
    )
    k = len(lines)
    return out[:k], out[k : 2 * k], out[2 * k :]


def split(values):
    high = values.astype(jnp.bfloat16)
    return high, (values - high.astype(jnp.float32)).astype(jnp.bfloat16)


def times(stack, values):
    half = stack.shape[0] // 2
    high, low = split(values)
    dot = functools.partial(jnp.dot, preferred_element_type=jnp.float32)
    first = dot(stack, high)
    return first[:half] + first[half:] + dot(stack[:half], low)


def put_taps(taps, group, at, writers):
    for j, targets in enumerate(writers):
        for ref, plane in targets:
            ref[plane, at : at + group, :] = taps[j * group : (j + 1) * group]


def writers_of(outs, near_at=0, away_at=0):
    near, away = outs
    return [[(near, 4 * near_at + j)] for j in range(4)] + [[(away, 2 * away_at + j)] for j in range(2)]


OUT_PLANES = (4, 2)


def along_y(stack, read, count_z, count_y, write, writers):
    group = min(count_z, DEPTH // count_y)
    for at in range(0, count_z, group):
        values = read(slice(at, at + group), slice(0, count_y))
        result = times(stack, values.reshape(group * count_y, -1))
        write(slice(at, at + group), slice(0, count_y), result[: group * count_y].reshape(values.shape))
        put_taps(result[group * count_y :], group, at, writers)


def along_z(stack, read, count_z, count_y, write, writers):
    group = min(count_y, DEPTH // count_z)
    for at in range(0, count_y, group):
        values = read(slice(0, count_z), slice(at, at + group))
        result = times(stack, values.reshape(count_z * group, -1))
        write(slice(0, count_z), slice(at, at + group), result[: count_z * group].reshape(values.shape))
        put_taps(result[count_z * group :], group, at, writers)


def flux_kernel(lines, blocks_y, blocks_z, pos_ref, v_ref, dy_ref, dz_ref, constants_ref, t_ref, *refs):
    count_c, count_z, count_y, _ = v_ref.shape
    *tables, ly_ref, lz_ref = refs[-6:]
    outs = list(refs[:-6])

    @pl.when(pl.program_id(0) == 0)
    def _():
        prepare_derivatives(
            lines, pos_ref, (dy_ref, dz_ref), constants_ref, (ly_ref, lz_ref), tables[:2], tables[2:]
        )

    for c in range(count_c):

        def write_y(zs, ys, value, c=c):
            t_ref[c, zs, ys] = v_ref[c, zs, ys] + value

        def write_z(zs, ys, value, c=c):
            t_ref[c, zs, ys] += value

        flux = lambda k: lambda zs, ys: v_ref[c, zs, ys] * v_ref[k, zs, ys]
        y_writers = writers_of((outs[c], outs[count_c]), 0, c)
        z_writers = writers_of(outs[count_c + 1 :], c, c)
        along_y(ly_ref[...], flux(1), count_z, count_y, write_y, y_writers)
        along_z(lz_ref[...], flux(2), count_z, count_y, write_z, z_writers)


def ends_of(chain_ref, blocks, planes):
    merged, count = table_counts(blocks)
    weight = lambda i, j: chain_ref[merged + i * count + j : merged + i * count + j + 1, :]
    return [sum(weight(i, j) * plane for j, plane in enumerate(planes)) for i in range(2)]


def spans(width):
    return [slice(x, x + SPAN) for x in range(0, width, SPAN)]


def far_planes(parts, blocks, xs):
    near, away, *rest = parts
    far = [(near, 2), (near, 3)] + ([(away, 2), (away, 3)] if blocks == 4 else [])
    far += [(ref, j) for ref in rest for j in range(2)]
    return [ref[j, :, xs] for ref, j in far]


def mend_y(read, write, chain_ref, table_ref, parts, blocks, ends_ref, dims):
    count_z, count_y, width = dims
    near, away = parts[:2]
    for xs in spans(width):
        ends_ref[0], ends_ref[1] = ends_of(chain_ref, blocks, far_planes(parts, blocks, xs))
        for y in range(0, count_y, 8):
            ys = slice(y, y + 8)
            column = [table_ref[j, ys, :] for j in range(6)]
            for z in range(count_z):
                at = slice(z, z + 1)
                value = read(z, ys, xs) + column[0] * ends_ref[0, at, :] + column[1] * ends_ref[1, at, :]
                if y == 0 or y == count_y - 8:
                    value = value + column[2] * near[0, at, xs] + column[3] * near[1, at, xs]
                    value = value + column[4] * away[0, at, xs] + column[5] * away[1, at, xs]
                write(z, ys, xs, value)


def mend_z(read, write, chain_ref, table_ref, parts, blocks, count_z, width):
    near, away = parts[:2]
    for xs in spans(width):
        g, h = ends_of(chain_ref, blocks, far_planes(parts, blocks, xs))
        for z in range(count_z):
            factor = [table_ref[j, z : z + 1, :] for j in range(6)]
            value = read(z, xs) + factor[0] * g + factor[1] * h
            if z in (0, count_z - 1):
                value = value + factor[2] * near[0, :, xs] + factor[4] * away[0, :, xs]
            if z in (1, count_z - 2):
                value = value + factor[3] * near[1, :, xs] + factor[5] * away[1, :, xs]
            write(z, xs, value)


def advance_kernel(blocks_y, blocks_z, *refs):
    refs = list(refs)
    take = lambda n: [refs.pop(0) for _ in range(n)]
    t_ref, lz_ref, cy_ref, cz_ref, sy_ref, sz_ref = take(6)
    y_parts, z_parts = take(part_count(blocks_y)), take(part_count(blocks_z))
    (out_ref,) = take(1)
    outs = take(len(OUT_PLANES))
    whole, ends = take(2)
    _, count_z, count_y, width = t_ref.shape

    def store_y(z, ys, xs, value):
        whole[z, ys, xs] = value

    def store_z(z, xs, value):
        whole[z, :, xs] = value

    def write(zs, ys, value):
        out_ref[zs, ys] = value

    dims = (count_z, count_y, width)
    mend_y(lambda z, ys, xs: t_ref[0, z, ys, xs], store_y, cy_ref, sy_ref, y_parts, blocks_y, ends, dims)
    mend_z(lambda z, xs: whole[z, :, xs], store_z, cz_ref, sz_ref, z_parts, blocks_z, count_z, width)
    along_z(lz_ref[...], lambda zs, ys: whole[zs, ys], count_z, count_y, write, writers_of(outs))


def filter_kernel(blocks_y, blocks_z, aliased, *refs):
    refs = list(refs)
    take = lambda n: [refs.pop(0) for _ in range(n)]
    t_ref, ly_ref, cz_ref, sz_ref = take(4)
    z_parts = take(part_count(blocks_z))
    take(aliased)
    (out_ref,) = take(1)
    outs = take(len(OUT_PLANES))
    (whole,) = take(1)
    count_z, count_y, width = t_ref.shape

    def store_z(z, xs, value):
        whole[z, :, xs] = value

    def write(zs, ys, value):
        out_ref[zs, ys] = value

    mend_z(lambda z, xs: t_ref[z, :, xs], store_z, cz_ref, sz_ref, z_parts, blocks_z, count_z, width)
    along_y(ly_ref[...], lambda zs, ys: whole[zs, ys], count_z, count_y, write, writers_of(outs))


def split_once(matrix_ref, high_ref, low_ref, factor):
    @pl.when(pl.program_id(0) == 0)
    def _():
        count = matrix_ref.shape[0]
        step = min(count, 128)
        for at in range(0, count, step):
            high_ref[at : at + step], low_ref[at : at + step] = split(matrix_ref[at : at + step] * factor)


def cut(array, start, count):
    whole = array.shape[1]
    start = start % whole
    if start + count <= whole:
        return array[:, start : start + count]
    return jnp.concatenate([array[:, start:], array[:, : start + count - whole]], axis=1)


def rows_times(values, high_ref, low_ref, write):
    high, low = split(values)
    dot = lambda x, w: lax.dot_general(x, w, (((1,), (1,)), ((), ())), preferred_element_type=jnp.float32)
    width = values.shape[1]
    for at in range(0, width, TILE):
        near = min(width, 2 * TILE)
        start = at - TILE // 2
        w_high, w_low = high_ref[at : at + TILE, :], low_ref[at : at + TILE, :]
        x_near, w_near = cut(high, start, near), cut(w_high, start, near)
        total = dot(x_near, w_near) + (dot(cut(low, start, near), w_near) + dot(x_near, cut(w_low, start, near)))
        if near < width:
            total = total + dot(cut(high, start + near, width - near), cut(w_high, start + near, width - near))
        write(slice(at, at + TILE), total)


def flux_x_kernel(v_ref, t_ref, matrix_ref, out_ref, high_ref, low_ref):
    split_once(matrix_ref, high_ref, low_ref, -STEP)
    values = v_ref[...] * v_ref[0:1]

    def write(xs, value):
        out_ref[:, :, :, xs] = t_ref[:, :, :, xs] + value.reshape(values.shape[:3] + (-1,))

    rows_times(values.reshape(-1, values.shape[-1]), high_ref, low_ref, write)


def last_kernel(blocks_y, aliased, *refs):
    refs = list(refs)
    take = lambda n: [refs.pop(0) for _ in range(n)]
    t_ref, matrix_ref, cy_ref, sy_ref = take(4)
    y_parts = take(part_count(blocks_y))
    take(aliased)
    (out_ref,) = take(1)
    whole, ends, high_ref, low_ref = take(4)
    count_z, count_y, width = t_ref.shape
    split_once(matrix_ref, high_ref, low_ref, 1.0)

    def store_y(z, ys, xs, value):
        whole[z, ys, xs] = value

    dims = (count_z, count_y, width)
    mend_y(lambda z, ys, xs: t_ref[z, ys, xs], store_y, cy_ref, sy_ref, y_parts, blocks_y, ends, dims)

    def write(xs, value):
        out_ref[0, :, :, xs] = value.reshape((count_z, count_y, -1))

    rows_times(whole[...].reshape(-1, width), high_ref, low_ref, write)


def merge_kernel(first_row, chain_ref, own_ref, other_ref, *refs):
    *extra, out_ref = refs
    high = own_ref.shape[0] // max(1, out_ref.shape[0] // 4)
    skip = 2 if extra else 0
    for c in range(out_ref.shape[0] // (2 + skip)):
        for ref in extra:
            out_ref[4 * c : 4 * c + 2] = ref[2 * c : 2 * c + 2]
        start = c * high + high - 2
        for xs in spans(out_ref.shape[2]):
            planes = [ref[start + j, :, xs] for ref in (own_ref, other_ref) for j in range(2)]
            for i in range(2):
                row = first_row + 4 * i
                out_ref[(2 + skip) * c + skip + i, :, xs] = sum(
                    chain_ref[row + j : row + j + 1, :] * plane for j, plane in enumerate(planes)
                )


def params(mib):
    return pltpu.CompilerParams(vmem_limit_bytes=mib * MIB)


def shape_of(*dims):
    return jax.ShapeDtypeStruct(dims, jnp.float32)


SMEM = pl.BlockSpec(memory_space=pltpu.SMEM)
VMEM = pl.BlockSpec(memory_space=pltpu.VMEM)


def part_count(blocks):
    return 2 if blocks == 4 else blocks.bit_length()


def hbm_of(*dims):
    return pltpu.HBM(dims, jnp.float32)


def vmem_of(*dims):
    return pltpu.VMEM(dims, jnp.float32)


class Order:
    def __init__(self):
        self.token = jnp.zeros((8, SPAN), jnp.float32)

    def call(self, kernel, operands, in_specs, out_specs, out_shape, carry=(), aliases=None, **kwargs):
        carry = [self.token, *carry]
        n_in, n_out, k = len(operands), len(out_shape), len(carry)
        aliases = dict(aliases or {})
        aliases.update({n_in + i: n_out + i for i in range(k)})

        def body(*refs):
            kernel(*refs[:n_in], *refs[n_in + k : n_in + k + n_out], *refs[n_in + 2 * k + n_out :])

        untouched = [pl.BlockSpec(memory_space=pl.ANY)] * k
        out = pl.pallas_call(
            body,
            in_specs=list(in_specs) + untouched,
            out_specs=list(out_specs) + untouched,
            out_shape=list(out_shape) + [hbm_of(*a.shape) for a in carry],
            input_output_aliases=aliases,
            **kwargs,
        )(*operands, *carry)
        self.token = out[n_out]
        return list(out[:n_out]), list(out[n_out + 1 :])


def whole_spec(array):
    return pl.BlockSpec(array.shape, lambda *_: (0,) * array.ndim)


def lane_spec(dims):
    return pl.BlockSpec(tuple(dims) + (LANES,), lambda i: (0,) * len(dims) + (i,))


def cost(flops, size):
    return pl.CostEstimate(flops=WEIGHT * int(flops), bytes_accessed=WEIGHT * int(size), transcendentals=0)


def flux_call(order, pos, velocity, matrices, lines, blocks_y, blocks_z):
    nc, nz, ny, width = velocity.shape
    size = nc * nz * ny * width
    constants, setup = derivative_constants(matrices, lines)
    planes = [(4, nz)] * nc + [(2 * nc, nz), (4 * nc, ny), (2 * nc, ny)]
    tables = [(6, n, SPAN) for n, _, _, _ in lines]
    tables += [(merged + 2 * count, SPAN) for merged, count in map(table_counts, (blocks_y, blocks_z))]
    constant = lambda dims: pl.BlockSpec(dims, lambda i: (0,) * len(dims))
    out, _ = order.call(
        functools.partial(flux_kernel, setup, blocks_y, blocks_z),
        [pos, velocity, *matrices, constants],
        [SMEM, lane_spec((nc, nz, ny))] + [whole_spec(a) for a in (*matrices, constants)],
        [lane_spec((nc, nz, ny))] + [lane_spec(dims) for dims in planes] + [constant(dims) for dims in tables],
        [hbm_of(nc, nz, ny, width)]
        + [hbm_of(*dims, width) for dims in planes]
        + [hbm_of(*dims) for dims in tables],
        grid=(width // LANES,),
        scratch_shapes=[pltpu.VMEM(stack_shape(n, group).shape, jnp.bfloat16) for n, group, _, _ in lines],
        compiler_params=params(64),
        cost_estimate=cost(size * 2 * 256 * 8, size * 9),
        name="flux_yz",
    )
    count = 1 + len(planes)
    return out[0], out[1:count], out[count:]


def flux_x_call(order, velocity, t, matrix, part, parts, carry):
    nc, nz, ny, width = velocity.shape
    group = max(1, min(nz // parts, ROWS // ny))
    steps = nz // parts // group
    block = pl.BlockSpec((nc, group, ny, width), lambda i: (0, part * steps + i, 0, 0))
    size = nc * nz * ny * width // parts
    (out,), carry = order.call(
        flux_x_kernel,
        [velocity, t, matrix],
        [block, block, whole_spec(matrix)],
        [block],
        [hbm_of(nc, nz, ny, width)],
        carry,
        {1: 0},
        grid=(steps,),
        scratch_shapes=[pltpu.VMEM(matrix.shape, jnp.bfloat16)] * 2,
        compiler_params=params(64),
        cost_estimate=cost(size * 4 * width, size * 13),
        name="flux_x",
    )
    return out, carry


def advance_call(order, t, c, lz, cy, cz, sy, sz, y_parts, z_parts, blocks_y, blocks_z, carry):
    _, nz, ny, width = t.shape
    size = nz * ny * width
    planes = list(y_parts) + list(z_parts)
    outs = [(k, ny) for k in OUT_PLANES]
    component = pl.BlockSpec((1, nz, ny, LANES), lambda i: (c, 0, 0, i))
    return order.call(
        functools.partial(advance_kernel, blocks_y, blocks_z),
        [t, lz, cy, cz, sy, sz] + [p.array for p in planes],
        [component] + [whole_spec(a) for a in (lz, cy, cz, sy, sz)] + [p.lane_spec() for p in planes],
        [lane_spec((nz, ny))] + [lane_spec(dims) for dims in outs],
        [vmem_of(nz, ny, width)] + [hbm_of(*dims, width) for dims in outs],
        carry,
        grid=(width // LANES,),
        scratch_shapes=[pltpu.VMEM((nz, ny, LANES), jnp.float32), pltpu.VMEM((2, nz, SPAN), jnp.float32)],
        compiler_params=params(ADVANCE_MIB),
        cost_estimate=cost(size * 2 * 256 * 4, size * 9),
        name="advance_z",
    )


def filter_call(order, t, c, count_c, ly, cz, sz, z_parts, whole, blocks_y, blocks_z):
    nz, ny, width = t.shape
    size = nz * ny * width
    aliased = [] if whole is None else [whole]
    operands = [t, ly, cz, sz] + [p.array for p in z_parts] + aliased
    out, _ = order.call(
        functools.partial(filter_kernel, blocks_y, blocks_z, len(aliased)),
        operands,
        [lane_spec((nz, ny))]
        + [whole_spec(a) for a in (ly, cz, sz)]
        + [p.lane_spec() for p in z_parts]
        + [pl.BlockSpec(memory_space=pl.ANY)] * len(aliased),
        [lane_spec((nz, ny)), lane_spec((4, nz)), pl.BlockSpec((2, nz, LANES), lambda i: (c, 0, i))],
        [vmem_of(nz, ny, width), hbm_of(4, nz, width), hbm_of(2 * count_c, nz, width)],
        (),
        {len(operands) - 1: 2} if aliased else {},
        grid=(width // LANES,),
        scratch_shapes=[pltpu.VMEM((nz, ny, LANES), jnp.float32)],
        compiler_params=params(SMALL_MIB),
        cost_estimate=cost(size * 2 * 256 * 4, size * 9),
        name="filter_y",
    )
    return out


def last_call(order, whole, t, c, count_c, matrix, cy, sy, y_parts, blocks_y):
    nz, ny, width = t.shape
    group = max(8, min(nz, DEPTH // ny))
    block = pl.BlockSpec((group, ny, width), lambda i: (i, 0, 0))
    size = nz * ny * width
    aliased = [] if whole is None else [whole]
    operands = [t, matrix, cy, sy] + [p.array for p in y_parts] + aliased
    (out,), _ = order.call(
        functools.partial(last_kernel, blocks_y, len(aliased)),
        operands,
        [block]
        + [whole_spec(a) for a in (matrix, cy, sy)]
        + [p.row_spec(group) for p in y_parts]
        + [pl.BlockSpec(memory_space=pl.ANY)] * len(aliased),
        [pl.BlockSpec((1, group, ny, width), lambda i: (c, i, 0, 0))],
        [hbm_of(count_c, nz, ny, width)],
        (),
        {len(operands) - 1: 0} if aliased else {},
        grid=(nz // group,),
        scratch_shapes=[pltpu.VMEM((group, ny, width), jnp.float32), pltpu.VMEM((2, group, SPAN), jnp.float32)]
        + [pltpu.VMEM(matrix.shape, jnp.bfloat16)] * 2,
        compiler_params=params(SMALL_MIB),
        cost_estimate=cost(size * 6 * width, size * 13),
        name="filter_x",
    )
    return out


class Planes:
    def __init__(self, array, count, index=0):
        self.array, self.count, self.index = array, count, index

    def lane_spec(self):
        return pl.BlockSpec((self.count, self.array.shape[1], LANES), lambda i: (self.index, 0, i))

    def row_spec(self, group):
        return pl.BlockSpec((self.count, group, self.array.shape[2]), lambda i: (self.index, i, 0))


def merge_call(order, chain, first_row, own, other, extra=(), carry=()):
    planes, lines, width = own.shape
    count = planes if extra else 2
    size = count * lines * width
    if extra:
        ends = whole_spec
    else:
        ends = lambda a: pl.BlockSpec((2, lines, width), lambda i: (a.shape[0] // 2 - 1, 0, 0))
    (out,), carry = order.call(
        functools.partial(merge_kernel, first_row),
        [chain, own, other, *extra],
        [whole_spec(chain), ends(own), ends(other)] + [whole_spec(a) for a in extra],
        [pl.BlockSpec((count, lines, width), lambda i: (0, 0, 0))],
        [hbm_of(count, lines, width)],
        carry,
        grid=(1,),
        compiler_params=params(SMALL_MIB),
        cost_estimate=cost(size * 8, size * 12),
        name="merge",
    )
    return out, carry


def send(axis, array, target):
    blocks = lax.axis_size(axis)
    return lax.ppermute(array, axis, [(i, target(i) % blocks) for i in range(blocks)])


def partner(i):
    return i ^ 1


def other_neighbour(i):
    return i - 1 if i % 2 == 0 else i + 1


class Exchange:
    def __init__(self, order, axis, near, chain, away=None):
        self.order, self.axis, self.own, self.chain, self.away = order, axis, near, chain, away
        self.blocks = lax.axis_size(axis)
        self.steps = 1 if self.blocks == 4 else self.blocks.bit_length() - 2
        self.far = []

    def begin(self):
        self.near = self.last = send(self.axis, self.own, partner)

    def step(self, carry=()):
        if len(self.far) == self.steps:
            return carry
        if self.blocks == 4:
            both, carry = merge_call(self.order, self.chain, 0, self.own, self.last, [self.away], carry)
            self.far = [send(self.axis, both, other_neighbour)]
            return carry
        level = len(self.far) + 1
        self.own, carry = merge_call(self.order, self.chain, 8 * (level - 1), self.own, self.last, (), carry)
        self.last = send(self.axis, self.own, lambda i: i ^ (1 << level))
        self.far.append(self.last)
        return carry

    def finish(self):
        while len(self.far) < self.steps:
            self.step()

    def parts(self, away, c, near_at=0):
        self.finish()
        if self.blocks == 4:
            return [Planes(self.near, 4, near_at), Planes(self.far[0], 4, near_at)]
        return [Planes(self.near, 4, near_at), Planes(away, 2, c)] + [Planes(array, 2) for array in self.far]


def on_device(velocity, derivative_x, derivative_y, derivative_z, smoothing_x, smoothing_y, smoothing_z):
    num_row, num_col = lax.axis_size("row"), lax.axis_size("col")
    pos = jnp.stack([lax.axis_index("row"), lax.axis_index("col")]).astype(jnp.int32)
    count_c, nz, ny, _ = velocity.shape
    lines = ((ny, min(nz, DEPTH // ny), False, num_row), (nz, min(ny, DEPTH // nz), True, num_col))
    order = Order()

    flux, outs, (dy, dz, cy, cz) = flux_call(
        order, pos, velocity, (derivative_y, derivative_z), lines, num_row, num_col
    )
    *y_near, y_away, z_near, z_away = outs
    four = num_col == 4
    if four:
        z_ex = [Exchange(order, "col", z_near, cz, z_away)]
        z_ex[0].begin()
    else:
        cut_near = lambda c: lax.slice_in_dim(z_near, 4 * c, 4 * c + 4)
        z_ex = [Exchange(order, "col", cut_near(c), cz) for c in range(count_c)]
        for ex in z_ex:
            ex.begin()
    y_ex = [Exchange(order, "row", near, cy) for near in y_near]
    y_ex[0].begin()
    flux, (y_ex[1].own, y_ex[2].own, y_away) = flux_x_call(
        order, velocity, flux, derivative_x, 0, 2, [y_ex[1].own, y_ex[2].own, y_away]
    )
    y_ex[0].step()
    y_ex[1].begin()
    for ex in z_ex:
        (y_away,) = ex.step([y_away])
        ex.finish()
    y_came = send("row", y_away, other_neighbour)
    flux, (y_ex[2].own,) = flux_x_call(order, velocity, flux, derivative_x, 1, 2, [y_ex[2].own])
    y_ex[0].step()
    y_ex[1].step()
    y_ex[2].begin()
    (my, mz), (sy, sz), (fy, fz) = smoothing_call(order, pos, (smoothing_y, smoothing_z), lines)
    y_ex[1].step()
    y_ex[2].step()
    z_came = None if four else send("col", z_away, other_neighbour)

    t_z, t_y = [None] * count_c, [None] * count_c
    f_ex = [None] * count_c
    g_ex = [None] * count_c
    z_back = [None] * count_c

    def advance(c):
        y_parts = y_ex[c].parts(y_came, c)
        z_parts = z_ex[0].parts(None, c, c) if four else z_ex[c].parts(z_came, c)
        (t_z[c], near, away), _ = advance_call(
            order, flux, c, mz, cy, cz, dy, dz, y_parts, z_parts, num_row, num_col, []
        )
        f_ex[c] = Exchange(order, "col", near, fz, away if four else None)
        f_ex[c].begin()
        z_back[c] = None if four else send("col", away, other_neighbour)

    def filter_yz(c, whole):
        z_parts = f_ex[c].parts(z_back[c], 0)
        t_y[c], near, whole = filter_call(
            order, t_z[c], c, count_c, my, fz, sz, z_parts, whole, num_row, num_col
        )
        g_ex[c] = Exchange(order, "row", near, fy)
        g_ex[c].begin()
        return whole

    advance(0)
    y_ex[2].step()
    advance(1)
    f_ex[0].step()
    advance(2)
    f_ex[1].step()
    whole = filter_yz(0, None)
    f_ex[2].step()
    whole = filter_yz(1, whole)
    g_ex[0].step()
    whole = filter_yz(2, whole)
    g_ex[1].step()
    (whole,) = g_ex[0].step([whole])
    came = send("row", whole, other_neighbour)
    g_ex[2].step()
    g_ex[1].step()
    out = None
    for c in range(count_c):
        y_parts = g_ex[c].parts(came, c)
        out = last_call(order, out, t_y[c], c, count_c, smoothing_x, fy, sy, y_parts, num_row)
        if c == 0:
            g_ex[2].step()
    return out


def solution(mesh):
    in_specs = (P(None, "col", "row", None), P(), P(), P(), P(), P(), P())
    out_specs = P(None, "col", "row", None)
    return jax.shard_map(
        on_device, mesh=mesh, in_specs=in_specs, out_specs=out_specs, check_vma=False
    )
```

```python
import functools

import jax
import jax.numpy as jnp
import numpy as np
from jax import lax
from jax.experimental import pallas as pl
from jax.experimental.pallas import tpu as pltpu
from jax.sharding import PartitionSpec as P

STEP = 0.1
PADE = 9.0 / 20.0
PADE_STENCIL = (63.0 / 80.0, 9.0 / 100.0, -7.0 / 1200.0)
SPAN = 128
LANES = 256
DEPTH = 256
ROWS = 128
TILE = 256
MIB = 1024 * 1024
SMALL_MIB = 24
ADVANCE_MIB = 50
WEIGHT = 1000


def numpy_lanes(blocks):
    index = np.arange(SPAN)[None, :]

    def flip(value, level):
        return value[:, index[0] ^ (1 << level)]

    def pick(level, own_right, own_left):
        return np.where((index >> level) & 1 == 1, own_right, own_left)

    return flip, pick


def kernel_lanes(blocks):
    index = lax.broadcasted_iota(jnp.int32, (1, SPAN), 1)

    def pick(level, own_right, own_left):
        return jnp.where((index >> level) & 1 == 1, own_right, own_left)

    def flip(value, level):
        step = 1 << level
        return pick(level, pltpu.roll(value, step, 1), pltpu.roll(value, SPAN - step, 1))

    return flip, pick


def chain_tables(flip, pick, alpha, beta, gamma, delta, blocks):
    levels = blocks.bit_length() - 1
    zero = alpha * 0.0
    unit = zero + 1.0
    width = 2 * levels

    def combine(terms):
        terms = list(terms)
        return [sum(c * v[j] for c, v in terms) for j in range(width)]

    def spot(at):
        return [unit if j == at else zero for j in range(width)]

    def choose(level, own_right, own_left):
        return [pick(level, r, l) for r, l in zip(own_right, own_left)]

    coefs = [alpha, beta, gamma, delta]
    h_own, k_own = [zero] * width, [zero] * width
    merges, saved = [], []
    for level in range(levels):
        sibling = [flip(value, level) for value in coefs]
        h_sib, k_sib = spot(2 * level), spot(2 * level + 1)
        saved.append((coefs, sibling, h_own, k_own, h_sib, k_sib))
        if level == levels - 1:
            break
        a1, b1, g1, d1 = choose(level, sibling, coefs)
        a2, b2, g2, d2 = choose(level, coefs, sibling)
        scale = 1.0 / (1.0 - d1 * a2)
        h_h2, h_k1 = b1 * scale, b1 * scale * a2
        k_k1, k_h2 = g2 * scale, g2 * scale * d1
        own_left = [unit, h_k1, h_h2, zero, zero, k_k1, k_h2, unit]
        own_right = [h_h2, zero, unit, h_k1, k_h2, unit, zero, k_k1]
        merge = choose(level, own_right, own_left)
        merges.append(merge)
        planes = (h_own, k_own, h_sib, k_sib)
        h_own, k_own = combine(zip(merge[:4], planes)), combine(zip(merge[4:], planes))
        coefs = [a1 + b1 * scale * a2 * g1, b1 * scale * b2, g2 * scale * g1, d2 + g2 * scale * d1 * b2]
    (ao, bo, go, do), (ab, bb, gb, db), h_o, k_o, h_b, k_b = saved[-1]
    m00 = 1.0 - (gb * go + db * ao)
    m01 = -(gb * do + db * bo)
    m10 = -(ab * go + bb * ao)
    m11 = 1.0 - (ab * do + bb * bo)
    inverse = 1.0 / (m00 * m11 - m01 * m10)
    right0 = combine([(unit, k_b), (gb, k_o), (db, h_o)])
    right1 = combine([(unit, h_b), (ab, k_o), (bb, h_o)])
    g_in = combine([(inverse * m11, right0), (-inverse * m01, right1)])
    h_in = combine([(inverse * m00, right1), (-inverse * m10, right0)])
    for level in range(levels - 2, -1, -1):
        (ao, bo, go, do), (ab, bb, gb, db), h_o, k_o, h_b, k_b = saved[level]
        left = 1.0 / (1.0 - do * ab)
        right = 1.0 / (1.0 - db * ao)
        h_left = combine([(left, h_b), (left * ab, k_o), (left * ab * go, g_in), (left * bb, h_in)])
        g_right = combine([(right, k_b), (right * gb, g_in), (right * db, h_o), (right * db * bo, h_in)])
        h_in, g_in = choose(level, h_in, h_left), choose(level, g_right, g_in)
    return sum(merges, []) + g_in + h_in


def table_counts(blocks):
    levels = blocks.bit_length() - 1
    return 8 * (levels - 1), 2 * levels


def end_rows(a_past, stencil_past, sign):
    a1, a2, a3 = a_past
    (p1, p2, p3), (_, q2, q3), (_, _, s3) = stencil_past
    zero = p1 * 0.0
    r1 = [sign * p1, sign * p2, sign * p3]
    r2 = [sign * q2, sign * q3, zero]
    w2 = [sign * s3 / a3, zero, zero]
    w1 = [(x - y) / a2 for x, y in zip(r2, w2)]
    w0 = [(x - y) / a1 - z for x, y, z in zip(r1, w1, w2)]
    return w0, w1, w2


def functionals(xp, index, a, a_left, a_right, stencils, symmetric, first_row, last_row):
    n = a.shape[0]
    low = 1.0 if symmetric else -1.0
    past = lambda rows: tuple(stencils(r)[1:] for r in rows)
    right = end_rows(a_right, past(a_right), low)
    left = end_rows(a_left, past(a_left), 1.0)
    at = lambda i, value: xp.where(index == i, value, 0.0)
    centre, *bands = stencils(a)

    def end(row):
        total = centre * row
        for k, band in enumerate(bands, 1):
            part = band * row
            edge = xp.zeros_like(part[:k])
            total = total + xp.concatenate([edge, part[:-k]], axis=0)
            total = total + low * xp.concatenate([part[k:], edge], axis=0)
        for i in range(3):
            moved = row[n - 1 : n] * (right[0][i] + a[n - 1 : n] * right[1][i]) + row[n - 2 : n - 1] * a[n - 2 : n - 1] * right[0][i]
            total = total - at(n - 1 - i, moved)
            moved = row[0:1] * (left[0][i] + a[0:1] * left[1][i]) + row[1:2] * a[1:2] * left[0][i]
            total = total - at(i, moved)
        return total

    tail = lambda w: sum(at(n - 1 - i, c) for i, c in enumerate(w))
    head = lambda w: sum(at(i, c) for i, c in enumerate(w))
    return [tail(right[1]), tail(right[2]), head(left[1]), head(left[2]), end(first_row), end(last_row)]


def pade_line(count, blocks):
    n = count // blocks
    full = np.eye(count) + PADE * (np.eye(count, k=1) + np.eye(count, k=-1))
    full[0, -1] = full[-1, 0] = PADE
    band = np.zeros((count, count))
    for k, c in enumerate(PADE_STENCIL, 1):
        band += c * (np.roll(np.eye(count), k, axis=1) - np.roll(np.eye(count), -k, axis=1))
    beside = np.linalg.solve(full, band)[0, 1]
    inside = np.linalg.inv(np.eye(n) + PADE * (np.eye(n, k=1) + np.eye(n, k=-1)))
    stencils = lambda a: [a * 0.0] + [a * 0.0 + c for c in PADE_STENCIL]
    side = [np.full((1, 1), PADE)] * 3
    index = np.arange(n)[:, None]
    taps = functionals(
        np, index, np.full((n, 1), PADE), side, side, stencils, False, inside[0][:, None], inside[-1][:, None]
    )
    spread = np.stack([-PADE * inside[:, 0], -PADE * inside[:, -1]], axis=1)
    every = lambda value: np.full((1, SPAN), value)
    flip, pick = numpy_lanes(blocks)
    table = chain_tables(
        flip, pick, every(spread[0, 0]), every(spread[0, 1]), every(spread[-1, 0]), every(spread[-1, 1]), blocks
    )
    return beside, np.concatenate(taps, axis=1), spread, np.concatenate(table, axis=0)


def exact_dot(x, y):
    return jnp.dot(x, y, precision=lax.Precision.HIGHEST, preferred_element_type=jnp.float32)


def iota(shape, axis):
    return lax.broadcasted_iota(jnp.int32, shape, axis)


def place_of(lane, n, group, inner):
    return (lane // group, lane % group) if inner else (lane % n, lane // n)


def block_rows(matrix_ref, block, n):
    return matrix_ref[pl.ds(pl.multiple_of(block * n, 8), n), :]


def store_stack(out_ref, rows, taps, block, n, group, inner):
    wide = n * group
    count = rows.shape[1]
    place, line = place_of(iota((1, wide), 1), n, group, inner)
    tiled = exact_dot(rows, (iota((count, wide), 0) == block * n + place).astype(jnp.float32))
    if inner:
        whole = jnp.broadcast_to(tiled[:, None, :], (n, group, wide)).reshape(wide, wide)
    else:
        whole = jnp.concatenate([tiled] * group, axis=0)
    _, row_line = place_of(iota((wide, 1), 0), n, group, inner)
    whole = jnp.where(row_line == line, whole, 0.0)
    mask = iota((group, wide), 0) == line
    both = jnp.concatenate([whole] + [jnp.where(mask, tap, 0.0) for tap in taps], axis=0)
    high = both.astype(jnp.bfloat16)
    half = both.shape[0]
    out_ref[:half] = high
    out_ref[half:] = (both - high.astype(jnp.float32)).astype(jnp.bfloat16)


def ordered(odd, taps):
    r1, r2, l1, l2, h, k = taps
    pick = lambda x, y: jnp.where(odd, x, y)
    return [pick(l1, r1), pick(l2, r2), h, k, pick(r1, l1), pick(r2, l2)]


def store_table(out_ref, odd, spread, factor):
    _, n, lanes = out_ref.shape
    row = iota((n, lanes), 0)
    side = odd.astype(jnp.int32)
    for j in range(2):
        out_ref[j] = jnp.broadcast_to(spread[j] * factor, (n, lanes))
        for k, first in enumerate((side, 1 - side)):
            spot = row == first * j + (1 - first) * (n - 1 - j)
            out_ref[2 + 2 * k + j] = jnp.where(spot, factor, 0.0)


def store_chain(out_ref, rows, block):
    own = jnp.sum(jnp.where(iota(rows.shape, 1) == block, rows, 0.0), axis=1, keepdims=True)
    out_ref[...] = jnp.broadcast_to(own, out_ref.shape)


def prepare_derivatives(lines, pos_ref, matrices, constants_ref, stacks, tables, chains):
    for axis, (n, group, inner, beside, (tap_at, spread_at, chain_at, chain_rows)) in enumerate(lines):
        block = pos_ref[axis]
        odd = block % 2 == 1
        rows = block_rows(matrices[axis], block, n)
        count = rows.shape[1]
        next_one = iota((n, count), 1) == (block * n + iota((n, count), 0) + 1) % count
        metric = jnp.sum(jnp.where(next_one, rows, 0.0), axis=1, keepdims=True) * (1.0 / beside)
        taps = [constants_ref[tap_at + j : tap_at + j + 1, : n * group] for j in range(6)]
        store_stack(stacks[axis], -STEP * rows, ordered(odd, taps), block, n, group, inner)
        spread = [constants_ref[spread_at : spread_at + n, j : j + 1] for j in range(2)]
        store_table(tables[axis], odd, spread, -STEP * metric)
        store_chain(chains[axis], constants_ref[chain_at : chain_at + chain_rows, :SPAN], block)


def filter_stencils(a):
    return [
        11.0 / 16.0 + 5.0 / 8.0 * a,
        15.0 / 64.0 + 17.0 / 32.0 * a,
        -3.0 / 32.0 + 3.0 / 16.0 * a,
        1.0 / 64.0 - 1.0 / 32.0 * a,
    ]


def block_ends(a, out_ref):
    n = a.shape[0]
    a = [a[i : i + 1, :] for i in range(n)]
    down, up = [jnp.ones_like(a[0])], [jnp.ones_like(a[0])]
    for i in range(1, n):
        down.append(1.0 / (1.0 - a[i] * a[i - 1] * down[i - 1]))
        j = n - 1 - i
        up.insert(0, 1.0 / (1.0 - a[j] * a[j + 1] * up[0]))
    column = row = up[0]
    out_ref[0, 0:1, :] = column
    out_ref[2, 0:1, :] = row
    for i in range(1, n):
        column = -a[i] * up[i] * column
        row = -a[i - 1] * up[i] * row
        out_ref[0, i : i + 1, :] = column
        out_ref[2, i : i + 1, :] = row
    column = row = down[-1]
    out_ref[1, n - 1 : n, :] = column
    out_ref[3, n - 1 : n, :] = row
    for i in range(n - 2, -1, -1):
        column = -a[i] * down[i] * column
        row = -a[i + 1] * down[i] * row
        out_ref[1, i : i + 1, :] = column
        out_ref[3, i : i + 1, :] = row


def smoothing_kernel(lines, pos_ref, *refs):
    refs = list(refs)
    take = lambda k: [refs.pop(0) for _ in range(k)]
    matrices = take(len(lines))
    stacks, tables, chains = take(len(lines)), take(len(lines)), take(len(lines))
    scratch = take(len(lines))
    for axis, (n, group, inner, blocks) in enumerate(lines):
        block = pos_ref[axis]
        odd = block % 2 == 1
        matrix = matrices[axis][...]
        count = matrix.shape[0]
        row, lane = iota((count, count), 0), iota((count, count), 1)
        middle = jnp.sum(jnp.where(row == lane, matrix, 0.0), axis=0, keepdims=True)
        near = (row == (lane + 1) % count) | (lane == (row + 1) % count)
        beside = jnp.sum(jnp.where(near, matrix, 0.0), axis=0, keepdims=True)
        along = (11.0 / 16.0 - middle) / (beside - 5.0 / 8.0)
        sorted_out = jnp.where(iota((n, count), 1) % n == iota((n, count), 0), along, 0.0)
        a = exact_dot(sorted_out, (iota((count, SPAN), 0) // n == iota((count, SPAN), 1)).astype(jnp.float32))
        ends_ref = scratch[axis]
        block_ends(a, ends_ref)
        column0, column1, row0, row1 = (ends_ref[j] for j in range(4))
        first, last = a[0:1], a[n - 1 : n]
        spread = [-first * column0, -last * column1]
        flip, pick = kernel_lanes(blocks)
        chain = chain_tables(
            flip, pick, spread[0][0:1], spread[1][0:1], spread[0][n - 1 : n], spread[1][n - 1 : n], blocks
        )
        store_chain(chains[axis], jnp.concatenate(chain, axis=0), block)
        index = iota((1, SPAN), 1)
        after = lambda v: jnp.where(index == blocks - 1, pltpu.roll(v, blocks - 1, 1), pltpu.roll(v, SPAN - 1, 1))
        before = lambda v: jnp.where(index == 0, pltpu.roll(v, SPAN - blocks + 1, 1), pltpu.roll(v, 1, 1))
        a_right = [after(a[i : i + 1]) for i in range(3)]
        a_left = [before(a[n - 1 - i : n - i]) for i in range(3)]
        used = index < blocks
        a_right = [jnp.where(used, v, 0.44) for v in a_right]
        a_left = [jnp.where(used, v, 0.44) for v in a_left]
        taps = functionals(jnp, iota((n, SPAN), 0), a, a_left, a_right, filter_stencils, True, row0, row1)
        own = lambda v: jnp.sum(jnp.where(iota((n, SPAN), 1) == block, v, 0.0), axis=1, keepdims=True)
        wide = n * group
        place, _ = place_of(iota((1, wide), 1), n, group, inner)
        at_place = iota((n, wide), 0) == place
        tap_rows = [jnp.sum(jnp.where(at_place, own(t), 0.0), axis=0, keepdims=True) for t in taps]
        rows = block_rows(matrices[axis], block, n)
        store_stack(stacks[axis], rows, ordered(odd, tap_rows), block, n, group, inner)
        store_table(tables[axis], odd, [own(s) for s in spread], jnp.ones((n, 1), jnp.float32))


def stack_shape(n, group):
    return jax.ShapeDtypeStruct((2 * group * (n + 6), group * n), jnp.bfloat16)


def derivative_constants(matrices, lines):
    rows, setup, at = [], [], 0

    def add(value):
        nonlocal at
        start = at
        high = -(-value.shape[0] // 8) * 8
        rows.append(np.pad(value, ((0, high - value.shape[0]), (0, DEPTH - value.shape[1]))))
        at += high
        return start

    for matrix, (n, group, inner, blocks) in zip(matrices, lines):
        beside, taps, spread, table = pade_line(matrix.shape[0], blocks)
        place, _ = place_of(np.arange(n * group), n, group, inner)
        where = (add(taps[place].T), add(spread), add(table), table.shape[0])
        setup.append((n, group, inner, beside, where))
    return jnp.asarray(np.concatenate(rows, axis=0).astype(np.float32)), setup


def smoothing_call(order, pos, matrices, lines):
    rows = [merged + 2 * planes for merged, planes in (table_counts(blocks) for _, _, _, blocks in lines)]
    out, _ = order.call(
        functools.partial(smoothing_kernel, lines),
        [pos, *matrices],
        [SMEM] + [VMEM] * len(lines),
        [VMEM] * (3 * len(lines)),
        [stack_shape(n, group) for n, group, _, _ in lines]
        + [shape_of(6, n, SPAN) for n, _, _, _ in lines]
        + [shape_of(r, SPAN) for r in rows],
        scratch_shapes=[pltpu.VMEM((4, n, SPAN), jnp.float32) for n, _, _, _ in lines],
        compiler_params=params(SMALL_MIB),
        cost_estimate=cost(10**7, 10**7),
        name="smoothing_lines",
    )
    k = len(lines)
    return out[:k], out[k : 2 * k], out[2 * k :]


def split(values):
    high = values.astype(jnp.bfloat16)
    return high, (values - high.astype(jnp.float32)).astype(jnp.bfloat16)


def times(stack, values):
    half = stack.shape[0] // 2
    high, low = split(values)
    dot = functools.partial(jnp.dot, preferred_element_type=jnp.float32)
    first = dot(stack, high)
    return first[:half] + first[half:] + dot(stack[:half], low)


def put_taps(taps, group, at, writers):
    for j, targets in enumerate(writers):
        for ref, plane in targets:
            ref[plane, at : at + group, :] = taps[j * group : (j + 1) * group]


def writers_of(outs, near_at=0, away_at=0):
    near, away = outs
    return [[(near, 4 * near_at + j)] for j in range(4)] + [[(away, 2 * away_at + j)] for j in range(2)]


OUT_PLANES = (4, 2)


def along_y(stack, read, count_z, count_y, write, writers):
    group = min(count_z, DEPTH // count_y)
    for at in range(0, count_z, group):
        values = read(slice(at, at + group), slice(0, count_y))
        result = times(stack, values.reshape(group * count_y, -1))
        write(slice(at, at + group), slice(0, count_y), result[: group * count_y].reshape(values.shape))
        put_taps(result[group * count_y :], group, at, writers)


def along_z(stack, read, count_z, count_y, write, writers):
    group = min(count_y, DEPTH // count_z)
    for at in range(0, count_y, group):
        values = read(slice(0, count_z), slice(at, at + group))
        result = times(stack, values.reshape(count_z * group, -1))
        write(slice(0, count_z), slice(at, at + group), result[: count_z * group].reshape(values.shape))
        put_taps(result[count_z * group :], group, at, writers)


def flux_kernel(lines, blocks_y, blocks_z, pos_ref, v_ref, dy_ref, dz_ref, constants_ref, t_ref, *refs):
    count_c, count_z, count_y, _ = v_ref.shape
    *tables, ly_ref, lz_ref = refs[-6:]
    outs = list(refs[:-6])

    @pl.when(pl.program_id(0) == 0)
    def _():
        prepare_derivatives(
            lines, pos_ref, (dy_ref, dz_ref), constants_ref, (ly_ref, lz_ref), tables[:2], tables[2:]
        )

    for c in range(count_c):

        def write_y(zs, ys, value, c=c):
            t_ref[c, zs, ys] = v_ref[c, zs, ys] + value

        def write_z(zs, ys, value, c=c):
            t_ref[c, zs, ys] += value

        flux = lambda k: lambda zs, ys: v_ref[c, zs, ys] * v_ref[k, zs, ys]
        y_writers = writers_of((outs[c], outs[count_c]), 0, c)
        z_writers = writers_of(outs[count_c + 1 :], c, c)
        along_y(ly_ref[...], flux(1), count_z, count_y, write_y, y_writers)
        along_z(lz_ref[...], flux(2), count_z, count_y, write_z, z_writers)


def ends_of(chain_ref, blocks, planes):
    merged, count = table_counts(blocks)
    weight = lambda i, j: chain_ref[merged + i * count + j : merged + i * count + j + 1, :]
    return [sum(weight(i, j) * plane for j, plane in enumerate(planes)) for i in range(2)]


def spans(width):
    return [slice(x, x + SPAN) for x in range(0, width, SPAN)]


def far_planes(parts, blocks, xs):
    near, away, *rest = parts
    far = [(near, 2), (near, 3)] + ([(away, 2), (away, 3)] if blocks == 4 else [])
    far += [(ref, j) for ref in rest for j in range(2)]
    return [ref[j, :, xs] for ref, j in far]


def mend_y(read, write, chain_ref, table_ref, parts, blocks, ends_ref, dims):
    count_z, count_y, width = dims
    near, away = parts[:2]
    for xs in spans(width):
        ends_ref[0], ends_ref[1] = ends_of(chain_ref, blocks, far_planes(parts, blocks, xs))
        for y in range(0, count_y, 8):
            ys = slice(y, y + 8)
            column = [table_ref[j, ys, :] for j in range(6)]
            for z in range(count_z):
                at = slice(z, z + 1)
                value = read(z, ys, xs) + column[0] * ends_ref[0, at, :] + column[1] * ends_ref[1, at, :]
                if y == 0 or y == count_y - 8:
                    value = value + column[2] * near[0, at, xs] + column[3] * near[1, at, xs]
                    value = value + column[4] * away[0, at, xs] + column[5] * away[1, at, xs]
                write(z, ys, xs, value)


def mend_z(read, write, chain_ref, table_ref, parts, blocks, count_z, width):
    near, away = parts[:2]
    for xs in spans(width):
        g, h = ends_of(chain_ref, blocks, far_planes(parts, blocks, xs))
        for z in range(count_z):
            factor = [table_ref[j, z : z + 1, :] for j in range(6)]
            value = read(z, xs) + factor[0] * g + factor[1] * h
            if z in (0, count_z - 1):
                value = value + factor[2] * near[0, :, xs] + factor[4] * away[0, :, xs]
            if z in (1, count_z - 2):
                value = value + factor[3] * near[1, :, xs] + factor[5] * away[1, :, xs]
            write(z, xs, value)


def advance_kernel(blocks_y, blocks_z, *refs):
    refs = list(refs)
    take = lambda n: [refs.pop(0) for _ in range(n)]
    t_ref, lz_ref, cy_ref, cz_ref, sy_ref, sz_ref = take(6)
    y_parts, z_parts = take(part_count(blocks_y)), take(part_count(blocks_z))
    (out_ref,) = take(1)
    outs = take(len(OUT_PLANES))
    whole, ends = take(2)
    _, count_z, count_y, width = t_ref.shape

    def store_y(z, ys, xs, value):
        whole[z, ys, xs] = value

    def store_z(z, xs, value):
        whole[z, :, xs] = value

    def write(zs, ys, value):
        out_ref[zs, ys] = value

    dims = (count_z, count_y, width)
    mend_y(lambda z, ys, xs: t_ref[0, z, ys, xs], store_y, cy_ref, sy_ref, y_parts, blocks_y, ends, dims)
    mend_z(lambda z, xs: whole[z, :, xs], store_z, cz_ref, sz_ref, z_parts, blocks_z, count_z, width)
    along_z(lz_ref[...], lambda zs, ys: whole[zs, ys], count_z, count_y, write, writers_of(outs))


def filter_kernel(blocks_y, blocks_z, aliased, *refs):
    refs = list(refs)
    take = lambda n: [refs.pop(0) for _ in range(n)]
    t_ref, ly_ref, cz_ref, sz_ref = take(4)
    z_parts = take(part_count(blocks_z))
    take(aliased)
    (out_ref,) = take(1)
    outs = take(len(OUT_PLANES))
    (whole,) = take(1)
    count_z, count_y, width = t_ref.shape

    def store_z(z, xs, value):
        whole[z, :, xs] = value

    def write(zs, ys, value):
        out_ref[zs, ys] = value

    mend_z(lambda z, xs: t_ref[z, :, xs], store_z, cz_ref, sz_ref, z_parts, blocks_z, count_z, width)
    along_y(ly_ref[...], lambda zs, ys: whole[zs, ys], count_z, count_y, write, writers_of(outs))


def split_once(matrix_ref, high_ref, low_ref, factor):
    @pl.when(pl.program_id(0) == 0)
    def _():
        count = matrix_ref.shape[0]
        step = min(count, 128)
        for at in range(0, count, step):
            high_ref[at : at + step], low_ref[at : at + step] = split(matrix_ref[at : at + step] * factor)


def cut(array, start, count):
    whole = array.shape[1]
    start = start % whole
    if start + count <= whole:
        return array[:, start : start + count]
    return jnp.concatenate([array[:, start:], array[:, : start + count - whole]], axis=1)


def rows_times(values, high_ref, low_ref, write):
    high, low = split(values)
    dot = lambda x, w: lax.dot_general(x, w, (((1,), (1,)), ((), ())), preferred_element_type=jnp.float32)
    width = values.shape[1]
    for at in range(0, width, TILE):
        near = min(width, 2 * TILE)
        start = at - TILE // 2
        w_high, w_low = high_ref[at : at + TILE, :], low_ref[at : at + TILE, :]
        x_near, w_near = cut(high, start, near), cut(w_high, start, near)
        total = dot(x_near, w_near) + (dot(cut(low, start, near), w_near) + dot(x_near, cut(w_low, start, near)))
        if near < width:
            total = total + dot(cut(high, start + near, width - near), cut(w_high, start + near, width - near))
        write(slice(at, at + TILE), total)


def flux_x_kernel(v_ref, t_ref, matrix_ref, out_ref, high_ref, low_ref):
    split_once(matrix_ref, high_ref, low_ref, -STEP)
    values = v_ref[...] * v_ref[0:1]

    def write(xs, value):
        out_ref[:, :, :, xs] = t_ref[:, :, :, xs] + value.reshape(values.shape[:3] + (-1,))

    rows_times(values.reshape(-1, values.shape[-1]), high_ref, low_ref, write)


def last_kernel(blocks_y, aliased, *refs):
    refs = list(refs)
    take = lambda n: [refs.pop(0) for _ in range(n)]
    t_ref, matrix_ref, cy_ref, sy_ref = take(4)
    y_parts = take(part_count(blocks_y))
    take(aliased)
    (out_ref,) = take(1)
    whole, ends, high_ref, low_ref = take(4)
    count_z, count_y, width = t_ref.shape
    split_once(matrix_ref, high_ref, low_ref, 1.0)

    def store_y(z, ys, xs, value):
        whole[z, ys, xs] = value

    dims = (count_z, count_y, width)
    mend_y(lambda z, ys, xs: t_ref[z, ys, xs], store_y, cy_ref, sy_ref, y_parts, blocks_y, ends, dims)

    def write(xs, value):
        out_ref[0, :, :, xs] = value.reshape((count_z, count_y, -1))

    rows_times(whole[...].reshape(-1, width), high_ref, low_ref, write)


def merge_kernel(first_row, chain_ref, own_ref, other_ref, *refs):
    *extra, out_ref = refs
    high = own_ref.shape[0] // max(1, out_ref.shape[0] // 4)
    skip = 2 if extra else 0
    for c in range(out_ref.shape[0] // (2 + skip)):
        for ref in extra:
            out_ref[4 * c : 4 * c + 2] = ref[2 * c : 2 * c + 2]
        start = c * high + high - 2
        for xs in spans(out_ref.shape[2]):
            planes = [ref[start + j, :, xs] for ref in (own_ref, other_ref) for j in range(2)]
            for i in range(2):
                row = first_row + 4 * i
                out_ref[(2 + skip) * c + skip + i, :, xs] = sum(
                    chain_ref[row + j : row + j + 1, :] * plane for j, plane in enumerate(planes)
                )


def params(mib):
    return pltpu.CompilerParams(vmem_limit_bytes=mib * MIB)


def shape_of(*dims):
    return jax.ShapeDtypeStruct(dims, jnp.float32)


SMEM = pl.BlockSpec(memory_space=pltpu.SMEM)
VMEM = pl.BlockSpec(memory_space=pltpu.VMEM)


def part_count(blocks):
    return 2 if blocks == 4 else blocks.bit_length()


def hbm_of(*dims):
    return pltpu.HBM(dims, jnp.float32)


def vmem_of(*dims):
    return pltpu.VMEM(dims, jnp.float32)


class Order:
    def __init__(self):
        self.token = jnp.zeros((8, SPAN), jnp.float32)

    def call(self, kernel, operands, in_specs, out_specs, out_shape, carry=(), aliases=None, **kwargs):
        carry = [self.token, *carry]
        n_in, n_out, k = len(operands), len(out_shape), len(carry)
        aliases = dict(aliases or {})
        aliases.update({n_in + i: n_out + i for i in range(k)})

        def body(*refs):
            kernel(*refs[:n_in], *refs[n_in + k : n_in + k + n_out], *refs[n_in + 2 * k + n_out :])

        untouched = [pl.BlockSpec(memory_space=pl.ANY)] * k
        out = pl.pallas_call(
            body,
            in_specs=list(in_specs) + untouched,
            out_specs=list(out_specs) + untouched,
            out_shape=list(out_shape) + [hbm_of(*a.shape) for a in carry],
            input_output_aliases=aliases,
            **kwargs,
        )(*operands, *carry)
        self.token = out[n_out]
        return list(out[:n_out]), list(out[n_out + 1 :])


def whole_spec(array):
    return pl.BlockSpec(array.shape, lambda *_: (0,) * array.ndim)


def lane_spec(dims):
    return pl.BlockSpec(tuple(dims) + (LANES,), lambda i: (0,) * len(dims) + (i,))


def cost(flops, size):
    return pl.CostEstimate(flops=WEIGHT * int(flops), bytes_accessed=WEIGHT * int(size), transcendentals=0)


def flux_call(order, pos, velocity, matrices, lines, blocks_y, blocks_z):
    nc, nz, ny, width = velocity.shape
    size = nc * nz * ny * width
    constants, setup = derivative_constants(matrices, lines)
    planes = [(4, nz)] * nc + [(2 * nc, nz), (4 * nc, ny), (2 * nc, ny)]
    tables = [(6, n, SPAN) for n, _, _, _ in lines]
    tables += [(merged + 2 * count, SPAN) for merged, count in map(table_counts, (blocks_y, blocks_z))]
    constant = lambda dims: pl.BlockSpec(dims, lambda i: (0,) * len(dims))
    out, _ = order.call(
        functools.partial(flux_kernel, setup, blocks_y, blocks_z),
        [pos, velocity, *matrices, constants],
        [SMEM, lane_spec((nc, nz, ny))] + [whole_spec(a) for a in (*matrices, constants)],
        [lane_spec((nc, nz, ny))] + [lane_spec(dims) for dims in planes] + [constant(dims) for dims in tables],
        [hbm_of(nc, nz, ny, width)]
        + [hbm_of(*dims, width) for dims in planes]
        + [hbm_of(*dims) for dims in tables],
        grid=(width // LANES,),
        scratch_shapes=[pltpu.VMEM(stack_shape(n, group).shape, jnp.bfloat16) for n, group, _, _ in lines],
        compiler_params=params(64),
        cost_estimate=cost(size * 2 * 256 * 8, size * 9),
        name="flux_yz",
    )
    count = 1 + len(planes)
    return out[0], out[1:count], out[count:]


def flux_x_call(order, velocity, t, matrix, part, parts, carry):
    nc, nz, ny, width = velocity.shape
    group = max(1, min(nz // parts, ROWS // ny))
    steps = nz // parts // group
    block = pl.BlockSpec((nc, group, ny, width), lambda i: (0, part * steps + i, 0, 0))
    size = nc * nz * ny * width // parts
    (out,), carry = order.call(
        flux_x_kernel,
        [velocity, t, matrix],
        [block, block, whole_spec(matrix)],
        [block],
        [hbm_of(nc, nz, ny, width)],
        carry,
        {1: 0},
        grid=(steps,),
        scratch_shapes=[pltpu.VMEM(matrix.shape, jnp.bfloat16)] * 2,
        compiler_params=params(64),
        cost_estimate=cost(size * 4 * width, size * 13),
        name="flux_x",
    )
    return out, carry


def advance_call(order, t, c, lz, cy, cz, sy, sz, y_parts, z_parts, blocks_y, blocks_z, carry):
    _, nz, ny, width = t.shape
    size = nz * ny * width
    planes = list(y_parts) + list(z_parts)
    outs = [(k, ny) for k in OUT_PLANES]
    component = pl.BlockSpec((1, nz, ny, LANES), lambda i: (c, 0, 0, i))
    return order.call(
        functools.partial(advance_kernel, blocks_y, blocks_z),
        [t, lz, cy, cz, sy, sz] + [p.array for p in planes],
        [component] + [whole_spec(a) for a in (lz, cy, cz, sy, sz)] + [p.lane_spec() for p in planes],
        [lane_spec((nz, ny))] + [lane_spec(dims) for dims in outs],
        [vmem_of(nz, ny, width)] + [hbm_of(*dims, width) for dims in outs],
        carry,
        grid=(width // LANES,),
        scratch_shapes=[pltpu.VMEM((nz, ny, LANES), jnp.float32), pltpu.VMEM((2, nz, SPAN), jnp.float32)],
        compiler_params=params(ADVANCE_MIB),
        cost_estimate=cost(size * 2 * 256 * 4, size * 9),
        name="advance_z",
    )


def filter_call(order, t, c, count_c, ly, cz, sz, z_parts, whole, blocks_y, blocks_z):
    nz, ny, width = t.shape
    size = nz * ny * width
    aliased = [] if whole is None else [whole]
    operands = [t, ly, cz, sz] + [p.array for p in z_parts] + aliased
    out, _ = order.call(
        functools.partial(filter_kernel, blocks_y, blocks_z, len(aliased)),
        operands,
        [lane_spec((nz, ny))]
        + [whole_spec(a) for a in (ly, cz, sz)]
        + [p.lane_spec() for p in z_parts]
        + [pl.BlockSpec(memory_space=pl.ANY)] * len(aliased),
        [lane_spec((nz, ny)), lane_spec((4, nz)), pl.BlockSpec((2, nz, LANES), lambda i: (c, 0, i))],
        [vmem_of(nz, ny, width), hbm_of(4, nz, width), hbm_of(2 * count_c, nz, width)],
        (),
        {len(operands) - 1: 2} if aliased else {},
        grid=(width // LANES,),
        scratch_shapes=[pltpu.VMEM((nz, ny, LANES), jnp.float32)],
        compiler_params=params(SMALL_MIB),
        cost_estimate=cost(size * 2 * 256 * 4, size * 9),
        name="filter_y",
    )
    return out


def last_call(order, whole, t, c, count_c, matrix, cy, sy, y_parts, blocks_y):
    nz, ny, width = t.shape
    group = max(8, min(nz, DEPTH // ny))
    block = pl.BlockSpec((group, ny, width), lambda i: (i, 0, 0))
    size = nz * ny * width
    aliased = [] if whole is None else [whole]
    operands = [t, matrix, cy, sy] + [p.array for p in y_parts] + aliased
    (out,), _ = order.call(
        functools.partial(last_kernel, blocks_y, len(aliased)),
        operands,
        [block]
        + [whole_spec(a) for a in (matrix, cy, sy)]
        + [p.row_spec(group) for p in y_parts]
        + [pl.BlockSpec(memory_space=pl.ANY)] * len(aliased),
        [pl.BlockSpec((1, group, ny, width), lambda i: (c, i, 0, 0))],
        [hbm_of(count_c, nz, ny, width)],
        (),
        {len(operands) - 1: 0} if aliased else {},
        grid=(nz // group,),
        scratch_shapes=[pltpu.VMEM((group, ny, width), jnp.float32), pltpu.VMEM((2, group, SPAN), jnp.float32)]
        + [pltpu.VMEM(matrix.shape, jnp.bfloat16)] * 2,
        compiler_params=params(SMALL_MIB),
        cost_estimate=cost(size * 6 * width, size * 13),
        name="filter_x",
    )
    return out


class Planes:
    def __init__(self, array, count, index=0):
        self.array, self.count, self.index = array, count, index

    def lane_spec(self):
        return pl.BlockSpec((self.count, self.array.shape[1], LANES), lambda i: (self.index, 0, i))

    def row_spec(self, group):
        return pl.BlockSpec((self.count, group, self.array.shape[2]), lambda i: (self.index, i, 0))


def merge_call(order, chain, first_row, own, other, extra=(), carry=()):
    planes, lines, width = own.shape
    count = planes if extra else 2
    size = count * lines * width
    if extra:
        ends = whole_spec
    else:
        ends = lambda a: pl.BlockSpec((2, lines, width), lambda i: (a.shape[0] // 2 - 1, 0, 0))
    (out,), carry = order.call(
        functools.partial(merge_kernel, first_row),
        [chain, own, other, *extra],
        [whole_spec(chain), ends(own), ends(other)] + [whole_spec(a) for a in extra],
        [pl.BlockSpec((count, lines, width), lambda i: (0, 0, 0))],
        [hbm_of(count, lines, width)],
        carry,
        grid=(1,),
        compiler_params=params(SMALL_MIB),
        cost_estimate=cost(size * 8, size * 12),
        name="merge",
    )
    return out, carry


def send(axis, array, target):
    blocks = lax.axis_size(axis)
    return lax.ppermute(array, axis, [(i, target(i) % blocks) for i in range(blocks)])


def partner(i):
    return i ^ 1


def other_neighbour(i):
    return i - 1 if i % 2 == 0 else i + 1


class Exchange:
    def __init__(self, order, axis, near, chain, away=None):
        self.order, self.axis, self.own, self.chain, self.away = order, axis, near, chain, away
        self.blocks = lax.axis_size(axis)
        self.steps = 1 if self.blocks == 4 else self.blocks.bit_length() - 2
        self.far = []

    def begin(self):
        self.near = self.last = send(self.axis, self.own, partner)

    def step(self, carry=()):
        if len(self.far) == self.steps:
            return carry
        if self.blocks == 4:
            both, carry = merge_call(self.order, self.chain, 0, self.own, self.last, [self.away], carry)
            self.far = [send(self.axis, both, other_neighbour)]
            return carry
        level = len(self.far) + 1
        self.own, carry = merge_call(self.order, self.chain, 8 * (level - 1), self.own, self.last, (), carry)
        self.last = send(self.axis, self.own, lambda i: i ^ (1 << level))
        self.far.append(self.last)
        return carry

    def finish(self):
        while len(self.far) < self.steps:
            self.step()

    def parts(self, away, c, near_at=0):
        self.finish()
        if self.blocks == 4:
            return [Planes(self.near, 4, near_at), Planes(self.far[0], 4, near_at)]
        return [Planes(self.near, 4, near_at), Planes(away, 2, c)] + [Planes(array, 2) for array in self.far]


def on_device(velocity, derivative_x, derivative_y, derivative_z, smoothing_x, smoothing_y, smoothing_z):
    num_row, num_col = lax.axis_size("row"), lax.axis_size("col")
    pos = jnp.stack([lax.axis_index("row"), lax.axis_index("col")]).astype(jnp.int32)
    count_c, nz, ny, _ = velocity.shape
    lines = ((ny, min(nz, DEPTH // ny), False, num_row), (nz, min(ny, DEPTH // nz), True, num_col))
    order = Order()

    flux, outs, (dy, dz, cy, cz) = flux_call(
        order, pos, velocity, (derivative_y, derivative_z), lines, num_row, num_col
    )
    *y_near, y_away, z_near, z_away = outs
    four = num_col == 4
    if four:
        z_ex = [Exchange(order, "col", z_near, cz, z_away)]
        z_ex[0].begin()
    else:
        cut_near = lambda c: lax.slice_in_dim(z_near, 4 * c, 4 * c + 4)
        z_ex = [Exchange(order, "col", cut_near(c), cz) for c in range(count_c)]
        for ex in z_ex:
            ex.begin()
    y_ex = [Exchange(order, "row", near, cy) for near in y_near]
    y_ex[0].begin()
    flux, (y_ex[1].own, y_ex[2].own, y_away) = flux_x_call(
        order, velocity, flux, derivative_x, 0, 2, [y_ex[1].own, y_ex[2].own, y_away]
    )
    y_ex[0].step()
    y_ex[1].begin()
    for ex in z_ex:
        y_away, y_ex[2].own = ex.step([y_away, y_ex[2].own])
        ex.finish()
    y_ex[2].begin()
    y_came = send("row", y_away, other_neighbour)
    flux, _ = flux_x_call(order, velocity, flux, derivative_x, 1, 2, [])
    y_ex[0].step()
    y_ex[1].step()
    y_ex[2].step()
    (my, mz), (sy, sz), (fy, fz) = smoothing_call(order, pos, (smoothing_y, smoothing_z), lines)
    y_ex[1].step()
    z_came = None if four else send("col", z_away, other_neighbour)

    t_z, t_y = [None] * count_c, [None] * count_c
    f_ex = [None] * count_c
    g_ex = [None] * count_c
    z_back = [None] * count_c

    def advance(c):
        y_parts = y_ex[c].parts(y_came, c)
        z_parts = z_ex[0].parts(None, c, c) if four else z_ex[c].parts(z_came, c)
        (t_z[c], near, away), _ = advance_call(
            order, flux, c, mz, cy, cz, dy, dz, y_parts, z_parts, num_row, num_col, []
        )
        f_ex[c] = Exchange(order, "col", near, fz, away if four else None)
        f_ex[c].begin()
        z_back[c] = None if four else send("col", away, other_neighbour)

    def filter_yz(c, whole):
        z_parts = f_ex[c].parts(z_back[c], 0)
        t_y[c], near, whole = filter_call(
            order, t_z[c], c, count_c, my, fz, sz, z_parts, whole, num_row, num_col
        )
        g_ex[c] = Exchange(order, "row", near, fy)
        g_ex[c].begin()
        return whole

    advance(0)
    y_ex[2].step()
    advance(1)
    f_ex[0].step()
    advance(2)
    f_ex[1].step()
    whole = filter_yz(0, None)
    f_ex[2].step()
    whole = filter_yz(1, whole)
    g_ex[0].step()
    whole = filter_yz(2, whole)
    came = send("row", whole, other_neighbour)
    g_ex[1].step()
    g_ex[0].step()
    g_ex[2].step()
    g_ex[1].step()
    out = None
    for c in range(count_c):
        y_parts = g_ex[c].parts(came, c)
        out = last_call(order, out, t_y[c], c, count_c, smoothing_x, fy, sy, y_parts, num_row)
        if c == 0:
            g_ex[2].step()
    return out


def solution(mesh):
    in_specs = (P(None, "col", "row", None), P(), P(), P(), P(), P(), P())
    out_specs = P(None, "col", "row", None)
    return jax.shard_map(
        on_device, mesh=mesh, in_specs=in_specs, out_specs=out_specs, check_vma=False
    )
```

```python
import functools

import jax
import jax.numpy as jnp
import numpy as np
from jax import lax
from jax.experimental import pallas as pl
from jax.experimental.pallas import tpu as pltpu
from jax.sharding import PartitionSpec as P

STEP = 0.1
PADE = 9.0 / 20.0
PADE_STENCIL = (63.0 / 80.0, 9.0 / 100.0, -7.0 / 1200.0)
SPAN = 128
LANES = 512
DEPTH = 256
ROWS = 128
TILE = 256
MIB = 1024 * 1024
SMALL_MIB = 24
ADVANCE_MIB = 50
WEIGHT = 1000


def numpy_lanes(blocks):
    index = np.arange(SPAN)[None, :]

    def flip(value, level):
        return value[:, index[0] ^ (1 << level)]

    def pick(level, own_right, own_left):
        return np.where((index >> level) & 1 == 1, own_right, own_left)

    return flip, pick


def kernel_lanes(blocks):
    index = lax.broadcasted_iota(jnp.int32, (1, SPAN), 1)

    def pick(level, own_right, own_left):
        return jnp.where((index >> level) & 1 == 1, own_right, own_left)

    def flip(value, level):
        step = 1 << level
        return pick(level, pltpu.roll(value, step, 1), pltpu.roll(value, SPAN - step, 1))

    return flip, pick


def chain_tables(flip, pick, alpha, beta, gamma, delta, blocks):
    levels = blocks.bit_length() - 1
    zero = alpha * 0.0
    unit = zero + 1.0
    width = 2 * levels

    def combine(terms):
        terms = list(terms)
        return [sum(c * v[j] for c, v in terms) for j in range(width)]

    def spot(at):
        return [unit if j == at else zero for j in range(width)]

    def choose(level, own_right, own_left):
        return [pick(level, r, l) for r, l in zip(own_right, own_left)]

    coefs = [alpha, beta, gamma, delta]
    h_own, k_own = [zero] * width, [zero] * width
    merges, saved = [], []
    for level in range(levels):
        sibling = [flip(value, level) for value in coefs]
        h_sib, k_sib = spot(2 * level), spot(2 * level + 1)
        saved.append((coefs, sibling, h_own, k_own, h_sib, k_sib))
        if level == levels - 1:
            break
        a1, b1, g1, d1 = choose(level, sibling, coefs)
        a2, b2, g2, d2 = choose(level, coefs, sibling)
        scale = 1.0 / (1.0 - d1 * a2)
        h_h2, h_k1 = b1 * scale, b1 * scale * a2
        k_k1, k_h2 = g2 * scale, g2 * scale * d1
        own_left = [unit, h_k1, h_h2, zero, zero, k_k1, k_h2, unit]
        own_right = [h_h2, zero, unit, h_k1, k_h2, unit, zero, k_k1]
        merge = choose(level, own_right, own_left)
        merges.append(merge)
        planes = (h_own, k_own, h_sib, k_sib)
        h_own, k_own = combine(zip(merge[:4], planes)), combine(zip(merge[4:], planes))
        coefs = [a1 + b1 * scale * a2 * g1, b1 * scale * b2, g2 * scale * g1, d2 + g2 * scale * d1 * b2]
    (ao, bo, go, do), (ab, bb, gb, db), h_o, k_o, h_b, k_b = saved[-1]
    m00 = 1.0 - (gb * go + db * ao)
    m01 = -(gb * do + db * bo)
    m10 = -(ab * go + bb * ao)
    m11 = 1.0 - (ab * do + bb * bo)
    inverse = 1.0 / (m00 * m11 - m01 * m10)
    right0 = combine([(unit, k_b), (gb, k_o), (db, h_o)])
    right1 = combine([(unit, h_b), (ab, k_o), (bb, h_o)])
    g_in = combine([(inverse * m11, right0), (-inverse * m01, right1)])
    h_in = combine([(inverse * m00, right1), (-inverse * m10, right0)])
    for level in range(levels - 2, -1, -1):
        (ao, bo, go, do), (ab, bb, gb, db), h_o, k_o, h_b, k_b = saved[level]
        left = 1.0 / (1.0 - do * ab)
        right = 1.0 / (1.0 - db * ao)
        h_left = combine([(left, h_b), (left * ab, k_o), (left * ab * go, g_in), (left * bb, h_in)])
        g_right = combine([(right, k_b), (right * gb, g_in), (right * db, h_o), (right * db * bo, h_in)])
        h_in, g_in = choose(level, h_in, h_left), choose(level, g_right, g_in)
    return sum(merges, []) + g_in + h_in


def table_counts(blocks):
    levels = blocks.bit_length() - 1
    return 8 * (levels - 1), 2 * levels


def end_rows(a_past, stencil_past, sign):
    a1, a2, a3 = a_past
    (p1, p2, p3), (_, q2, q3), (_, _, s3) = stencil_past
    zero = p1 * 0.0
    r1 = [sign * p1, sign * p2, sign * p3]
    r2 = [sign * q2, sign * q3, zero]
    w2 = [sign * s3 / a3, zero, zero]
    w1 = [(x - y) / a2 for x, y in zip(r2, w2)]
    w0 = [(x - y) / a1 - z for x, y, z in zip(r1, w1, w2)]
    return w0, w1, w2


def functionals(xp, index, a, a_left, a_right, stencils, symmetric, first_row, last_row):
    n = a.shape[0]
    low = 1.0 if symmetric else -1.0
    past = lambda rows: tuple(stencils(r)[1:] for r in rows)
    right = end_rows(a_right, past(a_right), low)
    left = end_rows(a_left, past(a_left), 1.0)
    at = lambda i, value: xp.where(index == i, value, 0.0)
    centre, *bands = stencils(a)

    def end(row):
        total = centre * row
        for k, band in enumerate(bands, 1):
            part = band * row
            edge = xp.zeros_like(part[:k])
            total = total + xp.concatenate([edge, part[:-k]], axis=0)
            total = total + low * xp.concatenate([part[k:], edge], axis=0)
        for i in range(3):
            moved = row[n - 1 : n] * (right[0][i] + a[n - 1 : n] * right[1][i]) + row[n - 2 : n - 1] * a[n - 2 : n - 1] * right[0][i]
            total = total - at(n - 1 - i, moved)
            moved = row[0:1] * (left[0][i] + a[0:1] * left[1][i]) + row[1:2] * a[1:2] * left[0][i]
            total = total - at(i, moved)
        return total

    tail = lambda w: sum(at(n - 1 - i, c) for i, c in enumerate(w))
    head = lambda w: sum(at(i, c) for i, c in enumerate(w))
    return [tail(right[1]), tail(right[2]), head(left[1]), head(left[2]), end(first_row), end(last_row)]


def pade_line(count, blocks):
    n = count // blocks
    full = np.eye(count) + PADE * (np.eye(count, k=1) + np.eye(count, k=-1))
    full[0, -1] = full[-1, 0] = PADE
    band = np.zeros((count, count))
    for k, c in enumerate(PADE_STENCIL, 1):
        band += c * (np.roll(np.eye(count), k, axis=1) - np.roll(np.eye(count), -k, axis=1))
    beside = np.linalg.solve(full, band)[0, 1]
    inside = np.linalg.inv(np.eye(n) + PADE * (np.eye(n, k=1) + np.eye(n, k=-1)))
    stencils = lambda a: [a * 0.0] + [a * 0.0 + c for c in PADE_STENCIL]
    side = [np.full((1, 1), PADE)] * 3
    index = np.arange(n)[:, None]
    taps = functionals(
        np, index, np.full((n, 1), PADE), side, side, stencils, False, inside[0][:, None], inside[-1][:, None]
    )
    spread = np.stack([-PADE * inside[:, 0], -PADE * inside[:, -1]], axis=1)
    every = lambda value: np.full((1, SPAN), value)
    flip, pick = numpy_lanes(blocks)
    table = chain_tables(
        flip, pick, every(spread[0, 0]), every(spread[0, 1]), every(spread[-1, 0]), every(spread[-1, 1]), blocks
    )
    return beside, np.concatenate(taps, axis=1), spread, np.concatenate(table, axis=0)


def exact_dot(x, y):
    return jnp.dot(x, y, precision=lax.Precision.HIGHEST, preferred_element_type=jnp.float32)


def iota(shape, axis):
    return lax.broadcasted_iota(jnp.int32, shape, axis)


def place_of(lane, n, group, inner):
    return (lane // group, lane % group) if inner else (lane % n, lane // n)


def block_rows(matrix_ref, block, n):
    return matrix_ref[pl.ds(pl.multiple_of(block * n, 8), n), :]


def store_stack(out_ref, rows, taps, block, n, group, inner):
    wide = n * group
    count = rows.shape[1]
    place, line = place_of(iota((1, wide), 1), n, group, inner)
    tiled = exact_dot(rows, (iota((count, wide), 0) == block * n + place).astype(jnp.float32))
    if inner:
        whole = jnp.broadcast_to(tiled[:, None, :], (n, group, wide)).reshape(wide, wide)
    else:
        whole = jnp.concatenate([tiled] * group, axis=0)
    _, row_line = place_of(iota((wide, 1), 0), n, group, inner)
    whole = jnp.where(row_line == line, whole, 0.0)
    mask = iota((group, wide), 0) == line
    both = jnp.concatenate([whole] + [jnp.where(mask, tap, 0.0) for tap in taps], axis=0)
    high = both.astype(jnp.bfloat16)
    half = both.shape[0]
    out_ref[:half] = high
    out_ref[half:] = (both - high.astype(jnp.float32)).astype(jnp.bfloat16)


def ordered(odd, taps):
    r1, r2, l1, l2, h, k = taps
    pick = lambda x, y: jnp.where(odd, x, y)
    return [pick(l1, r1), pick(l2, r2), h, k, pick(r1, l1), pick(r2, l2)]


def store_table(out_ref, odd, spread, factor):
    _, n, lanes = out_ref.shape
    row = iota((n, lanes), 0)
    side = odd.astype(jnp.int32)
    for j in range(2):
        out_ref[j] = jnp.broadcast_to(spread[j] * factor, (n, lanes))
        for k, first in enumerate((side, 1 - side)):
            spot = row == first * j + (1 - first) * (n - 1 - j)
            out_ref[2 + 2 * k + j] = jnp.where(spot, factor, 0.0)


def store_chain(out_ref, rows, block):
    own = jnp.sum(jnp.where(iota(rows.shape, 1) == block, rows, 0.0), axis=1, keepdims=True)
    out_ref[...] = jnp.broadcast_to(own, out_ref.shape)


def prepare_derivatives(lines, pos_ref, matrices, constants_ref, stacks, tables, chains):
    for axis, (n, group, inner, beside, (tap_at, spread_at, chain_at, chain_rows)) in enumerate(lines):
        block = pos_ref[axis]
        odd = block % 2 == 1
        rows = block_rows(matrices[axis], block, n)
        count = rows.shape[1]
        next_one = iota((n, count), 1) == (block * n + iota((n, count), 0) + 1) % count
        metric = jnp.sum(jnp.where(next_one, rows, 0.0), axis=1, keepdims=True) * (1.0 / beside)
        taps = [constants_ref[tap_at + j : tap_at + j + 1, : n * group] for j in range(6)]
        store_stack(stacks[axis], -STEP * rows, ordered(odd, taps), block, n, group, inner)
        spread = [constants_ref[spread_at : spread_at + n, j : j + 1] for j in range(2)]
        store_table(tables[axis], odd, spread, -STEP * metric)
        store_chain(chains[axis], constants_ref[chain_at : chain_at + chain_rows, :SPAN], block)


def filter_stencils(a):
    return [
        11.0 / 16.0 + 5.0 / 8.0 * a,
        15.0 / 64.0 + 17.0 / 32.0 * a,
        -3.0 / 32.0 + 3.0 / 16.0 * a,
        1.0 / 64.0 - 1.0 / 32.0 * a,
    ]


def block_ends(a, out_ref):
    n = a.shape[0]
    a = [a[i : i + 1, :] for i in range(n)]
    down, up = [jnp.ones_like(a[0])], [jnp.ones_like(a[0])]
    for i in range(1, n):
        down.append(1.0 / (1.0 - a[i] * a[i - 1] * down[i - 1]))
        j = n - 1 - i
        up.insert(0, 1.0 / (1.0 - a[j] * a[j + 1] * up[0]))
    column = row = up[0]
    out_ref[0, 0:1, :] = column
    out_ref[2, 0:1, :] = row
    for i in range(1, n):
        column = -a[i] * up[i] * column
        row = -a[i - 1] * up[i] * row
        out_ref[0, i : i + 1, :] = column
        out_ref[2, i : i + 1, :] = row
    column = row = down[-1]
    out_ref[1, n - 1 : n, :] = column
    out_ref[3, n - 1 : n, :] = row
    for i in range(n - 2, -1, -1):
        column = -a[i] * down[i] * column
        row = -a[i + 1] * down[i] * row
        out_ref[1, i : i + 1, :] = column
        out_ref[3, i : i + 1, :] = row


def smoothing_kernel(lines, pos_ref, *refs):
    refs = list(refs)
    take = lambda k: [refs.pop(0) for _ in range(k)]
    matrices = take(len(lines))
    stacks, tables, chains = take(len(lines)), take(len(lines)), take(len(lines))
    scratch = take(len(lines))
    for axis, (n, group, inner, blocks) in enumerate(lines):
        block = pos_ref[axis]
        odd = block % 2 == 1
        matrix = matrices[axis][...]
        count = matrix.shape[0]
        row, lane = iota((count, count), 0), iota((count, count), 1)
        middle = jnp.sum(jnp.where(row == lane, matrix, 0.0), axis=0, keepdims=True)
        near = (row == (lane + 1) % count) | (lane == (row + 1) % count)
        beside = jnp.sum(jnp.where(near, matrix, 0.0), axis=0, keepdims=True)
        along = (11.0 / 16.0 - middle) / (beside - 5.0 / 8.0)
        sorted_out = jnp.where(iota((n, count), 1) % n == iota((n, count), 0), along, 0.0)
        a = exact_dot(sorted_out, (iota((count, SPAN), 0) // n == iota((count, SPAN), 1)).astype(jnp.float32))
        ends_ref = scratch[axis]
        block_ends(a, ends_ref)
        column0, column1, row0, row1 = (ends_ref[j] for j in range(4))
        first, last = a[0:1], a[n - 1 : n]
        spread = [-first * column0, -last * column1]
        flip, pick = kernel_lanes(blocks)
        chain = chain_tables(
            flip, pick, spread[0][0:1], spread[1][0:1], spread[0][n - 1 : n], spread[1][n - 1 : n], blocks
        )
        store_chain(chains[axis], jnp.concatenate(chain, axis=0), block)
        index = iota((1, SPAN), 1)
        after = lambda v: jnp.where(index == blocks - 1, pltpu.roll(v, blocks - 1, 1), pltpu.roll(v, SPAN - 1, 1))
        before = lambda v: jnp.where(index == 0, pltpu.roll(v, SPAN - blocks + 1, 1), pltpu.roll(v, 1, 1))
        a_right = [after(a[i : i + 1]) for i in range(3)]
        a_left = [before(a[n - 1 - i : n - i]) for i in range(3)]
        used = index < blocks
        a_right = [jnp.where(used, v, 0.44) for v in a_right]
        a_left = [jnp.where(used, v, 0.44) for v in a_left]
        taps = functionals(jnp, iota((n, SPAN), 0), a, a_left, a_right, filter_stencils, True, row0, row1)
        own = lambda v: jnp.sum(jnp.where(iota((n, SPAN), 1) == block, v, 0.0), axis=1, keepdims=True)
        wide = n * group
        place, _ = place_of(iota((1, wide), 1), n, group, inner)
        at_place = iota((n, wide), 0) == place
        tap_rows = [jnp.sum(jnp.where(at_place, own(t), 0.0), axis=0, keepdims=True) for t in taps]
        rows = block_rows(matrices[axis], block, n)
        store_stack(stacks[axis], rows, ordered(odd, tap_rows), block, n, group, inner)
        store_table(tables[axis], odd, [own(s) for s in spread], jnp.ones((n, 1), jnp.float32))


def stack_shape(n, group):
    return jax.ShapeDtypeStruct((2 * group * (n + 6), group * n), jnp.bfloat16)


def derivative_constants(matrices, lines):
    rows, setup, at = [], [], 0

    def add(value):
        nonlocal at
        start = at
        high = -(-value.shape[0] // 8) * 8
        rows.append(np.pad(value, ((0, high - value.shape[0]), (0, DEPTH - value.shape[1]))))
        at += high
        return start

    for matrix, (n, group, inner, blocks) in zip(matrices, lines):
        beside, taps, spread, table = pade_line(matrix.shape[0], blocks)
        place, _ = place_of(np.arange(n * group), n, group, inner)
        where = (add(taps[place].T), add(spread), add(table), table.shape[0])
        setup.append((n, group, inner, beside, where))
    return jnp.asarray(np.concatenate(rows, axis=0).astype(np.float32)), setup


def smoothing_call(order, pos, matrices, lines):
    rows = [merged + 2 * planes for merged, planes in (table_counts(blocks) for _, _, _, blocks in lines)]
    out, _ = order.call(
        functools.partial(smoothing_kernel, lines),
        [pos, *matrices],
        [SMEM] + [VMEM] * len(lines),
        [VMEM] * (3 * len(lines)),
        [stack_shape(n, group) for n, group, _, _ in lines]
        + [shape_of(6, n, SPAN) for n, _, _, _ in lines]
        + [shape_of(r, SPAN) for r in rows],
        scratch_shapes=[pltpu.VMEM((4, n, SPAN), jnp.float32) for n, _, _, _ in lines],
        compiler_params=params(SMALL_MIB),
        cost_estimate=cost(10**7, 10**7),
        name="smoothing_lines",
    )
    k = len(lines)
    return out[:k], out[k : 2 * k], out[2 * k :]


def split(values):
    high = values.astype(jnp.bfloat16)
    return high, (values - high.astype(jnp.float32)).astype(jnp.bfloat16)


def times(stack, values):
    half = stack.shape[0] // 2
    high, low = split(values)
    dot = functools.partial(jnp.dot, preferred_element_type=jnp.float32)
    first = dot(stack, high)
    return first[:half] + first[half:] + dot(stack[:half], low)


def put_taps(taps, group, at, writers):
    for j, targets in enumerate(writers):
        for ref, plane in targets:
            ref[plane, at : at + group, :] = taps[j * group : (j + 1) * group]


def writers_of(outs, near_at=0, away_at=0):
    near, away = outs
    return [[(near, 4 * near_at + j)] for j in range(4)] + [[(away, 2 * away_at + j)] for j in range(2)]


OUT_PLANES = (4, 2)


def along_y(stack, read, count_z, count_y, write, writers):
    group = min(count_z, DEPTH // count_y)
    for at in range(0, count_z, group):
        values = read(slice(at, at + group), slice(0, count_y))
        result = times(stack, values.reshape(group * count_y, -1))
        write(slice(at, at + group), slice(0, count_y), result[: group * count_y].reshape(values.shape))
        put_taps(result[group * count_y :], group, at, writers)


def along_z(stack, read, count_z, count_y, write, writers):
    group = min(count_y, DEPTH // count_z)
    for at in range(0, count_y, group):
        values = read(slice(0, count_z), slice(at, at + group))
        result = times(stack, values.reshape(count_z * group, -1))
        write(slice(0, count_z), slice(at, at + group), result[: count_z * group].reshape(values.shape))
        put_taps(result[count_z * group :], group, at, writers)


def flux_kernel(lines, blocks_y, blocks_z, pos_ref, v_ref, dy_ref, dz_ref, constants_ref, t_ref, *refs):
    count_c, count_z, count_y, _ = v_ref.shape
    *tables, ly_ref, lz_ref = refs[-6:]
    outs = list(refs[:-6])

    @pl.when(pl.program_id(0) == 0)
    def _():
        prepare_derivatives(
            lines, pos_ref, (dy_ref, dz_ref), constants_ref, (ly_ref, lz_ref), tables[:2], tables[2:]
        )

    for c in range(count_c):

        def write_y(zs, ys, value, c=c):
            t_ref[c, zs, ys] = v_ref[c, zs, ys] + value

        def write_z(zs, ys, value, c=c):
            t_ref[c, zs, ys] += value

        flux = lambda k: lambda zs, ys: v_ref[c, zs, ys] * v_ref[k, zs, ys]
        y_writers = writers_of((outs[c], outs[count_c]), 0, c)
        z_writers = writers_of(outs[count_c + 1 :], c, c)
        along_y(ly_ref[...], flux(1), count_z, count_y, write_y, y_writers)
        along_z(lz_ref[...], flux(2), count_z, count_y, write_z, z_writers)


def ends_of(chain_ref, blocks, planes):
    merged, count = table_counts(blocks)
    weight = lambda i, j: chain_ref[merged + i * count + j : merged + i * count + j + 1, :]
    return [sum(weight(i, j) * plane for j, plane in enumerate(planes)) for i in range(2)]


def spans(width):
    return [slice(x, x + SPAN) for x in range(0, width, SPAN)]


def far_planes(parts, blocks, xs):
    near, away, *rest = parts
    far = [(near, 2), (near, 3)] + ([(away, 2), (away, 3)] if blocks == 4 else [])
    far += [(ref, j) for ref in rest for j in range(2)]
    return [ref[j, :, xs] for ref, j in far]


def mend_y(read, write, chain_ref, table_ref, parts, blocks, ends_ref, dims):
    count_z, count_y, width = dims
    near, away = parts[:2]
    for xs in spans(width):
        ends_ref[0], ends_ref[1] = ends_of(chain_ref, blocks, far_planes(parts, blocks, xs))
        for y in range(0, count_y, 8):
            ys = slice(y, y + 8)
            column = [table_ref[j, ys, :] for j in range(6)]
            for z in range(count_z):
                at = slice(z, z + 1)
                value = read(z, ys, xs) + column[0] * ends_ref[0, at, :] + column[1] * ends_ref[1, at, :]
                if y == 0 or y == count_y - 8:
                    value = value + column[2] * near[0, at, xs] + column[3] * near[1, at, xs]
                    value = value + column[4] * away[0, at, xs] + column[5] * away[1, at, xs]
                write(z, ys, xs, value)


def mend_z(read, write, chain_ref, table_ref, parts, blocks, count_z, width):
    near, away = parts[:2]
    for xs in spans(width):
        g, h = ends_of(chain_ref, blocks, far_planes(parts, blocks, xs))
        for z in range(count_z):
            factor = [table_ref[j, z : z + 1, :] for j in range(6)]
            value = read(z, xs) + factor[0] * g + factor[1] * h
            if z in (0, count_z - 1):
                value = value + factor[2] * near[0, :, xs] + factor[4] * away[0, :, xs]
            if z in (1, count_z - 2):
                value = value + factor[3] * near[1, :, xs] + factor[5] * away[1, :, xs]
            write(z, xs, value)


def advance_kernel(blocks_y, blocks_z, *refs):
    refs = list(refs)
    take = lambda n: [refs.pop(0) for _ in range(n)]
    t_ref, lz_ref, cy_ref, cz_ref, sy_ref, sz_ref = take(6)
    y_parts, z_parts = take(part_count(blocks_y)), take(part_count(blocks_z))
    (out_ref,) = take(1)
    outs = take(len(OUT_PLANES))
    whole, ends = take(2)
    _, count_z, count_y, width = t_ref.shape

    def store_y(z, ys, xs, value):
        whole[z, ys, xs] = value

    def store_z(z, xs, value):
        whole[z, :, xs] = value

    def write(zs, ys, value):
        out_ref[zs, ys] = value

    dims = (count_z, count_y, width)
    mend_y(lambda z, ys, xs: t_ref[0, z, ys, xs], store_y, cy_ref, sy_ref, y_parts, blocks_y, ends, dims)
    mend_z(lambda z, xs: whole[z, :, xs], store_z, cz_ref, sz_ref, z_parts, blocks_z, count_z, width)
    along_z(lz_ref[...], lambda zs, ys: whole[zs, ys], count_z, count_y, write, writers_of(outs))


def filter_kernel(blocks_y, blocks_z, aliased, *refs):
    refs = list(refs)
    take = lambda n: [refs.pop(0) for _ in range(n)]
    t_ref, ly_ref, cz_ref, sz_ref = take(4)
    z_parts = take(part_count(blocks_z))
    take(aliased)
    (out_ref,) = take(1)
    outs = take(len(OUT_PLANES))
    (whole,) = take(1)
    count_z, count_y, width = t_ref.shape

    def store_z(z, xs, value):
        whole[z, :, xs] = value

    def write(zs, ys, value):
        out_ref[zs, ys] = value

    mend_z(lambda z, xs: t_ref[z, :, xs], store_z, cz_ref, sz_ref, z_parts, blocks_z, count_z, width)
    along_y(ly_ref[...], lambda zs, ys: whole[zs, ys], count_z, count_y, write, writers_of(outs))


def split_once(matrix_ref, high_ref, low_ref, factor):
    @pl.when(pl.program_id(0) == 0)
    def _():
        count = matrix_ref.shape[0]
        step = min(count, 128)
        for at in range(0, count, step):
            high_ref[at : at + step], low_ref[at : at + step] = split(matrix_ref[at : at + step] * factor)


def cut(array, start, count):
    whole = array.shape[1]
    start = start % whole
    if start + count <= whole:
        return array[:, start : start + count]
    return jnp.concatenate([array[:, start:], array[:, : start + count - whole]], axis=1)


def rows_times(values, high_ref, low_ref, write):
    high, low = split(values)
    dot = lambda x, w: lax.dot_general(x, w, (((1,), (1,)), ((), ())), preferred_element_type=jnp.float32)
    width = values.shape[1]
    for at in range(0, width, TILE):
        near = min(width, 2 * TILE)
        start = at - TILE // 2
        w_high, w_low = high_ref[at : at + TILE, :], low_ref[at : at + TILE, :]
        x_near, w_near = cut(high, start, near), cut(w_high, start, near)
        total = dot(x_near, w_near) + (dot(cut(low, start, near), w_near) + dot(x_near, cut(w_low, start, near)))
        if near < width:
            total = total + dot(cut(high, start + near, width - near), cut(w_high, start + near, width - near))
        write(slice(at, at + TILE), total)


def flux_x_kernel(v_ref, t_ref, matrix_ref, out_ref, high_ref, low_ref):
    split_once(matrix_ref, high_ref, low_ref, -STEP)
    values = v_ref[...] * v_ref[0:1]

    def write(xs, value):
        out_ref[:, :, :, xs] = t_ref[:, :, :, xs] + value.reshape(values.shape[:3] + (-1,))

    rows_times(values.reshape(-1, values.shape[-1]), high_ref, low_ref, write)


def last_kernel(blocks_y, aliased, *refs):
    refs = list(refs)
    take = lambda n: [refs.pop(0) for _ in range(n)]
    t_ref, matrix_ref, cy_ref, sy_ref = take(4)
    y_parts = take(part_count(blocks_y))
    take(aliased)
    (out_ref,) = take(1)
    whole, ends, high_ref, low_ref = take(4)
    count_z, count_y, width = t_ref.shape
    split_once(matrix_ref, high_ref, low_ref, 1.0)

    def store_y(z, ys, xs, value):
        whole[z, ys, xs] = value

    dims = (count_z, count_y, width)
    mend_y(lambda z, ys, xs: t_ref[z, ys, xs], store_y, cy_ref, sy_ref, y_parts, blocks_y, ends, dims)

    def write(xs, value):
        out_ref[0, :, :, xs] = value.reshape((count_z, count_y, -1))

    rows_times(whole[...].reshape(-1, width), high_ref, low_ref, write)


def merge_kernel(first_row, chain_ref, own_ref, other_ref, *refs):
    *extra, out_ref = refs
    high = own_ref.shape[0] // max(1, out_ref.shape[0] // 4)
    skip = 2 if extra else 0
    for c in range(out_ref.shape[0] // (2 + skip)):
        for ref in extra:
            out_ref[4 * c : 4 * c + 2] = ref[2 * c : 2 * c + 2]
        start = c * high + high - 2
        for xs in spans(out_ref.shape[2]):
            planes = [ref[start + j, :, xs] for ref in (own_ref, other_ref) for j in range(2)]
            for i in range(2):
                row = first_row + 4 * i
                out_ref[(2 + skip) * c + skip + i, :, xs] = sum(
                    chain_ref[row + j : row + j + 1, :] * plane for j, plane in enumerate(planes)
                )


def params(mib):
    return pltpu.CompilerParams(vmem_limit_bytes=mib * MIB)


def shape_of(*dims):
    return jax.ShapeDtypeStruct(dims, jnp.float32)


SMEM = pl.BlockSpec(memory_space=pltpu.SMEM)
VMEM = pl.BlockSpec(memory_space=pltpu.VMEM)


def part_count(blocks):
    return 2 if blocks == 4 else blocks.bit_length()


def hbm_of(*dims):
    return pltpu.HBM(dims, jnp.float32)


def vmem_of(*dims):
    return pltpu.VMEM(dims, jnp.float32)


class Order:
    def __init__(self):
        self.token = jnp.zeros((8, SPAN), jnp.float32)

    def call(self, kernel, operands, in_specs, out_specs, out_shape, carry=(), aliases=None, **kwargs):
        carry = [self.token, *carry]
        n_in, n_out, k = len(operands), len(out_shape), len(carry)
        aliases = dict(aliases or {})
        aliases.update({n_in + i: n_out + i for i in range(k)})

        def body(*refs):
            kernel(*refs[:n_in], *refs[n_in + k : n_in + k + n_out], *refs[n_in + 2 * k + n_out :])

        untouched = [pl.BlockSpec(memory_space=pl.ANY)] * k
        out = pl.pallas_call(
            body,
            in_specs=list(in_specs) + untouched,
            out_specs=list(out_specs) + untouched,
            out_shape=list(out_shape) + [hbm_of(*a.shape) for a in carry],
            input_output_aliases=aliases,
            **kwargs,
        )(*operands, *carry)
        self.token = out[n_out]
        return list(out[:n_out]), list(out[n_out + 1 :])


def whole_spec(array):
    return pl.BlockSpec(array.shape, lambda *_: (0,) * array.ndim)


def lane_spec(dims):
    return pl.BlockSpec(tuple(dims) + (LANES,), lambda i: (0,) * len(dims) + (i,))


def cost(flops, size):
    return pl.CostEstimate(flops=WEIGHT * int(flops), bytes_accessed=WEIGHT * int(size), transcendentals=0)


def flux_call(order, pos, velocity, matrices, lines, blocks_y, blocks_z):
    nc, nz, ny, width = velocity.shape
    size = nc * nz * ny * width
    constants, setup = derivative_constants(matrices, lines)
    planes = [(4, nz)] * nc + [(2 * nc, nz), (4 * nc, ny), (2 * nc, ny)]
    tables = [(6, n, SPAN) for n, _, _, _ in lines]
    tables += [(merged + 2 * count, SPAN) for merged, count in map(table_counts, (blocks_y, blocks_z))]
    constant = lambda dims: pl.BlockSpec(dims, lambda i: (0,) * len(dims))
    out, _ = order.call(
        functools.partial(flux_kernel, setup, blocks_y, blocks_z),
        [pos, velocity, *matrices, constants],
        [SMEM, lane_spec((nc, nz, ny))] + [whole_spec(a) for a in (*matrices, constants)],
        [lane_spec((nc, nz, ny))] + [lane_spec(dims) for dims in planes] + [constant(dims) for dims in tables],
        [hbm_of(nc, nz, ny, width)]
        + [hbm_of(*dims, width) for dims in planes]
        + [hbm_of(*dims) for dims in tables],
        grid=(width // LANES,),
        scratch_shapes=[pltpu.VMEM(stack_shape(n, group).shape, jnp.bfloat16) for n, group, _, _ in lines],
        compiler_params=params(64),
        cost_estimate=cost(size * 2 * 256 * 8, size * 9),
        name="flux_yz",
    )
    count = 1 + len(planes)
    return out[0], out[1:count], out[count:]


def flux_x_call(order, velocity, t, matrix, part, parts, carry):
    nc, nz, ny, width = velocity.shape
    group = max(1, min(nz // parts, ROWS // ny))
    steps = nz // parts // group
    block = pl.BlockSpec((nc, group, ny, width), lambda i: (0, part * steps + i, 0, 0))
    size = nc * nz * ny * width // parts
    (out,), carry = order.call(
        flux_x_kernel,
        [velocity, t, matrix],
        [block, block, whole_spec(matrix)],
        [block],
        [hbm_of(nc, nz, ny, width)],
        carry,
        {1: 0},
        grid=(steps,),
        scratch_shapes=[pltpu.VMEM(matrix.shape, jnp.bfloat16)] * 2,
        compiler_params=params(64),
        cost_estimate=cost(size * 4 * width, size * 13),
        name="flux_x",
    )
    return out, carry


def advance_call(order, t, c, lz, cy, cz, sy, sz, y_parts, z_parts, blocks_y, blocks_z, carry):
    _, nz, ny, width = t.shape
    size = nz * ny * width
    planes = list(y_parts) + list(z_parts)
    outs = [(k, ny) for k in OUT_PLANES]
    component = pl.BlockSpec((1, nz, ny, LANES), lambda i: (c, 0, 0, i))
    return order.call(
        functools.partial(advance_kernel, blocks_y, blocks_z),
        [t, lz, cy, cz, sy, sz] + [p.array for p in planes],
        [component] + [whole_spec(a) for a in (lz, cy, cz, sy, sz)] + [p.lane_spec() for p in planes],
        [lane_spec((nz, ny))] + [lane_spec(dims) for dims in outs],
        [vmem_of(nz, ny, width)] + [hbm_of(*dims, width) for dims in outs],
        carry,
        grid=(width // LANES,),
        scratch_shapes=[pltpu.VMEM((nz, ny, LANES), jnp.float32), pltpu.VMEM((2, nz, SPAN), jnp.float32)],
        compiler_params=params(ADVANCE_MIB),
        cost_estimate=cost(size * 2 * 256 * 4, size * 9),
        name="advance_z",
    )


def filter_call(order, t, c, count_c, ly, cz, sz, z_parts, whole, blocks_y, blocks_z):
    nz, ny, width = t.shape
    size = nz * ny * width
    aliased = [] if whole is None else [whole]
    operands = [t, ly, cz, sz] + [p.array for p in z_parts] + aliased
    out, _ = order.call(
        functools.partial(filter_kernel, blocks_y, blocks_z, len(aliased)),
        operands,
        [lane_spec((nz, ny))]
        + [whole_spec(a) for a in (ly, cz, sz)]
        + [p.lane_spec() for p in z_parts]
        + [pl.BlockSpec(memory_space=pl.ANY)] * len(aliased),
        [lane_spec((nz, ny)), lane_spec((4, nz)), pl.BlockSpec((2, nz, LANES), lambda i: (c, 0, i))],
        [vmem_of(nz, ny, width), hbm_of(4, nz, width), hbm_of(2 * count_c, nz, width)],
        (),
        {len(operands) - 1: 2} if aliased else {},
        grid=(width // LANES,),
        scratch_shapes=[pltpu.VMEM((nz, ny, LANES), jnp.float32)],
        compiler_params=params(SMALL_MIB),
        cost_estimate=cost(size * 2 * 256 * 4, size * 9),
        name="filter_y",
    )
    return out


def last_call(order, whole, t, c, count_c, matrix, cy, sy, y_parts, blocks_y):
    nz, ny, width = t.shape
    group = max(8, min(nz, DEPTH // ny))
    block = pl.BlockSpec((group, ny, width), lambda i: (i, 0, 0))
    size = nz * ny * width
    aliased = [] if whole is None else [whole]
    operands = [t, matrix, cy, sy] + [p.array for p in y_parts] + aliased
    (out,), _ = order.call(
        functools.partial(last_kernel, blocks_y, len(aliased)),
        operands,
        [block]
        + [whole_spec(a) for a in (matrix, cy, sy)]
        + [p.row_spec(group) for p in y_parts]
        + [pl.BlockSpec(memory_space=pl.ANY)] * len(aliased),
        [pl.BlockSpec((1, group, ny, width), lambda i: (c, i, 0, 0))],
        [hbm_of(count_c, nz, ny, width)],
        (),
        {len(operands) - 1: 0} if aliased else {},
        grid=(nz // group,),
        scratch_shapes=[pltpu.VMEM((group, ny, width), jnp.float32), pltpu.VMEM((2, group, SPAN), jnp.float32)]
        + [pltpu.VMEM(matrix.shape, jnp.bfloat16)] * 2,
        compiler_params=params(SMALL_MIB),
        cost_estimate=cost(size * 6 * width, size * 13),
        name="filter_x",
    )
    return out


class Planes:
    def __init__(self, array, count, index=0):
        self.array, self.count, self.index = array, count, index

    def lane_spec(self):
        return pl.BlockSpec((self.count, self.array.shape[1], LANES), lambda i: (self.index, 0, i))

    def row_spec(self, group):
        return pl.BlockSpec((self.count, group, self.array.shape[2]), lambda i: (self.index, i, 0))


def merge_call(order, chain, first_row, own, other, extra=(), carry=()):
    planes, lines, width = own.shape
    count = planes if extra else 2
    size = count * lines * width
    if extra:
        ends = whole_spec
    else:
        ends = lambda a: pl.BlockSpec((2, lines, width), lambda i: (a.shape[0] // 2 - 1, 0, 0))
    (out,), carry = order.call(
        functools.partial(merge_kernel, first_row),
        [chain, own, other, *extra],
        [whole_spec(chain), ends(own), ends(other)] + [whole_spec(a) for a in extra],
        [pl.BlockSpec((count, lines, width), lambda i: (0, 0, 0))],
        [hbm_of(count, lines, width)],
        carry,
        grid=(1,),
        compiler_params=params(SMALL_MIB),
        cost_estimate=cost(size * 8, size * 12),
        name="merge",
    )
    return out, carry


def send(axis, array, target):
    blocks = lax.axis_size(axis)
    return lax.ppermute(array, axis, [(i, target(i) % blocks) for i in range(blocks)])


def partner(i):
    return i ^ 1


def other_neighbour(i):
    return i - 1 if i % 2 == 0 else i + 1


class Exchange:
    def __init__(self, order, axis, near, chain, away=None):
        self.order, self.axis, self.own, self.chain, self.away = order, axis, near, chain, away
        self.blocks = lax.axis_size(axis)
        self.steps = 1 if self.blocks == 4 else self.blocks.bit_length() - 2
        self.far = []

    def begin(self):
        self.near = self.last = send(self.axis, self.own, partner)

    def step(self, carry=()):
        if len(self.far) == self.steps:
            return carry
        if self.blocks == 4:
            both, carry = merge_call(self.order, self.chain, 0, self.own, self.last, [self.away], carry)
            self.far = [send(self.axis, both, other_neighbour)]
            return carry
        level = len(self.far) + 1
        self.own, carry = merge_call(self.order, self.chain, 8 * (level - 1), self.own, self.last, (), carry)
        self.last = send(self.axis, self.own, lambda i: i ^ (1 << level))
        self.far.append(self.last)
        return carry

    def finish(self):
        while len(self.far) < self.steps:
            self.step()

    def parts(self, away, c, near_at=0):
        self.finish()
        if self.blocks == 4:
            return [Planes(self.near, 4, near_at), Planes(self.far[0], 4, near_at)]
        return [Planes(self.near, 4, near_at), Planes(away, 2, c)] + [Planes(array, 2) for array in self.far]


def on_device(velocity, derivative_x, derivative_y, derivative_z, smoothing_x, smoothing_y, smoothing_z):
    num_row, num_col = lax.axis_size("row"), lax.axis_size("col")
    pos = jnp.stack([lax.axis_index("row"), lax.axis_index("col")]).astype(jnp.int32)
    count_c, nz, ny, _ = velocity.shape
    lines = ((ny, min(nz, DEPTH // ny), False, num_row), (nz, min(ny, DEPTH // nz), True, num_col))
    order = Order()

    flux, outs, (dy, dz, cy, cz) = flux_call(
        order, pos, velocity, (derivative_y, derivative_z), lines, num_row, num_col
    )
    *y_near, y_away, z_near, z_away = outs
    four = num_col == 4
    if four:
        z_ex = [Exchange(order, "col", z_near, cz, z_away)]
        z_ex[0].begin()
    else:
        cut_near = lambda c: lax.slice_in_dim(z_near, 4 * c, 4 * c + 4)
        z_ex = [Exchange(order, "col", cut_near(c), cz) for c in range(count_c)]
        for ex in z_ex:
            ex.begin()
    y_ex = [Exchange(order, "row", near, cy) for near in y_near]
    y_ex[0].begin()
    flux, (y_ex[1].own, y_ex[2].own, y_away) = flux_x_call(
        order, velocity, flux, derivative_x, 0, 2, [y_ex[1].own, y_ex[2].own, y_away]
    )
    y_ex[0].step()
    y_ex[1].begin()
    for ex in z_ex:
        y_away, y_ex[2].own = ex.step([y_away, y_ex[2].own])
        ex.finish()
    y_ex[2].begin()
    y_came = send("row", y_away, other_neighbour)
    flux, _ = flux_x_call(order, velocity, flux, derivative_x, 1, 2, [])
    y_ex[0].step()
    y_ex[1].step()
    y_ex[2].step()
    (my, mz), (sy, sz), (fy, fz) = smoothing_call(order, pos, (smoothing_y, smoothing_z), lines)
    y_ex[1].step()
    z_came = None if four else send("col", z_away, other_neighbour)

    t_z, t_y = [None] * count_c, [None] * count_c
    f_ex = [None] * count_c
    g_ex = [None] * count_c
    z_back = [None] * count_c

    def advance(c):
        y_parts = y_ex[c].parts(y_came, c)
        z_parts = z_ex[0].parts(None, c, c) if four else z_ex[c].parts(z_came, c)
        (t_z[c], near, away), _ = advance_call(
            order, flux, c, mz, cy, cz, dy, dz, y_parts, z_parts, num_row, num_col, []
        )
        f_ex[c] = Exchange(order, "col", near, fz, away if four else None)
        f_ex[c].begin()
        z_back[c] = None if four else send("col", away, other_neighbour)

    def filter_yz(c, whole):
        z_parts = f_ex[c].parts(z_back[c], 0)
        t_y[c], near, whole = filter_call(
            order, t_z[c], c, count_c, my, fz, sz, z_parts, whole, num_row, num_col
        )
        g_ex[c] = Exchange(order, "row", near, fy)
        g_ex[c].begin()
        return whole

    advance(0)
    y_ex[2].step()
    advance(1)
    f_ex[0].step()
    advance(2)
    f_ex[1].step()
    whole = filter_yz(0, None)
    f_ex[2].step()
    whole = filter_yz(1, whole)
    g_ex[0].step()
    whole = filter_yz(2, whole)
    came = send("row", whole, other_neighbour)
    g_ex[1].step()
    g_ex[0].step()
    g_ex[2].step()
    g_ex[1].step()
    out = None
    for c in range(count_c):
        y_parts = g_ex[c].parts(came, c)
        out = last_call(order, out, t_y[c], c, count_c, smoothing_x, fy, sy, y_parts, num_row)
        if c == 0:
            g_ex[2].step()
    return out


def solution(mesh):
    in_specs = (P(None, "col", "row", None), P(), P(), P(), P(), P(), P())
    out_specs = P(None, "col", "row", None)
    return jax.shard_map(
        on_device, mesh=mesh, in_specs=in_specs, out_specs=out_specs, check_vma=False
    )
```
